32 devices in a mesh: segment: 2 (over y), tm: 4 (over z), rows: 4 (over x, core).
Axes of the slice: x: 2, y: 2, z: 4, core: 2. Of those that a mesh axis runs over, the one named last changes fastest.
Arguments:
- input_clip: bfloat16 [8, 8, 128, 128], P('tm', 'rows'), may hold values from -6 to 6
- cotangent: bfloat16 [8, 8, 128, 128], P('tm', 'rows'), may hold values from -0.125 to 0.125
- kernel_in: bfloat16 [2, 3456, 256], P('segment'), may hold values from -0.109375 to 0.109375
- kernel_out: bfloat16 [2, 6912, 128], P('segment'), may hold values from -0.078125 to 0.078125
Outputs:
- sections: bfloat16 [2, 8, 8, 128, 128], P('segment', 'tm', 'rows')
- grad_in: float32 [2, 884736], P('segment', ('tm', 'rows'))
- grad_out: float32 [2, 884736], P('segment', ('tm', 'rows'))
The draws below stay inside these ranges and needn't reach their ends.
All inputs are finite; a program needn't handle non-finite values.
Results may differ from the reference program's by a relative error of at most 0.007.
Values may be sent and summed in bfloat16 or wider, within the bound.
No kernel may reach another device: no remote copies, remote signals or barrier semaphores. Data moves between devices by JAX's collectives and lax.ppermute only.
A program may use at most 128 MiB of HBM per device.

```python
import jax
import jax.numpy as jnp
from jax import lax

CH = 128
HID = 256
WID = 128
FRAMES = 8
HEIGHT = 8


def steps_of(rng, dims, split, low, largest):
    def one(axis_at, blocks):
        heights = jax.random.uniform(jax.random.fold_in(jax.random.fold_in(rng, 6), axis_at), (blocks,), jnp.float32, low / len(split), largest / len(split))
        return jnp.repeat(jnp.exp(heights), dims[axis_at] // blocks).reshape((-1,) + (1,) * (len(dims) - axis_at - 1))

    loudness = one(*split[0])
    for cut in split[1:]:
        loudness = loudness * one(*cut)
    return loudness


def centred(own_key, dims, scale, limit, cuts=(), held_as=jnp.bfloat16):
    gain = steps_of(own_key, dims, cuts, -0.22, 0.18) if cuts else 1.0
    array = jax.random.normal(own_key, dims, jnp.float32) * scale * gain
    return jnp.minimum(jnp.maximum(array, -limit), limit).astype(held_as)


def setup_inputs(seed: int = 0) -> dict:
    seeds = jax.random.split(jax.random.key(seed), 5)
    input_clip = centred(seeds[0], (FRAMES, HEIGHT, WID, CH), 1.0, 6.0, ((0, 4), (1, 4)))
    cotangent = centred(seeds[1], (FRAMES, HEIGHT, WID, CH), (2.0 / (FRAMES * HEIGHT * WID) ** 0.5), 0.125, ((0, 4), (1, 4)))
    kernel_in = centred(seeds[2], (2, 27 * CH, HID), (27 * CH) ** -0.5, 0.109375, ((0, 2),))
    kernel_out = centred(seeds[3], (2, 27 * HID, CH), (27 * HID) ** -0.5, 0.078125, ((0, 2),))
    return {"input_clip": input_clip, "cotangent": cotangent, "kernel_in": kernel_in, "kernel_out": kernel_out}


def causal_conv(volume, kernel):
    frames, height, width, channels = volume.shape
    padded = jnp.pad(volume, ((2, 0), (1, 1), (1, 1), (0, 0)))
    blocks = kernel.reshape(27, channels, -1)
    summed = jnp.zeros((frames * height * width, blocks.shape[2]), jnp.float32)
    for depth in range(3):
        for row_step in range(3):
            for col_step in range(3):
                window = padded[depth:depth + frames, row_step:row_step + height, col_step:col_step + width]
                summed = summed + jnp.dot(window.reshape(-1, channels), blocks[9 * depth + 3 * row_step + col_step], preferred_element_type=jnp.float32)
    return summed.reshape(frames, height, width, -1)

def conv_transpose(volume, kernel):
    frames, height, width, channels = volume.shape
    padded = jnp.pad(volume, ((0, 2), (1, 1), (1, 1), (0, 0)))
    blocks = kernel.reshape(27, -1, channels)
    summed = jnp.zeros((frames * height * width, blocks.shape[1]), jnp.float32)
    for depth in range(3):
        for row_step in range(3):
            for col_step in range(3):
                window = padded[2 - depth:2 - depth + frames, 2 - row_step:2 - row_step + height, 2 - col_step:2 - col_step + width]
                summed = summed + jnp.dot(window.reshape(-1, channels), blocks[9 * depth + 3 * row_step + col_step].T, preferred_element_type=jnp.float32)
    return summed.reshape(frames, height, width, -1)

def weight_grad(volume, upstream):
    frames, height, width, channels = volume.shape
    padded = jnp.pad(volume, ((2, 0), (1, 1), (1, 1), (0, 0)))
    flat_up = upstream.reshape(frames * height * width, -1)
    pieces = []
    for depth in range(3):
        for row_step in range(3):
            for col_step in range(3):
                window = padded[depth:depth + frames, row_step:row_step + height, col_step:col_step + width]
                pieces.append(lax.dot_general(window.reshape(-1, channels), flat_up, (((0,), (0,)), ((), ())), preferred_element_type=jnp.float32))
    return jnp.stack(pieces).reshape(-1)

def section(volume, kernel_a, kernel_b):
    hidden = causal_conv(volume, kernel_a)
    active = jax.nn.silu(hidden).astype(jnp.bfloat16)
    result = (volume.astype(jnp.float32) + causal_conv(active, kernel_b)).astype(jnp.bfloat16)
    return (result, hidden, active)

def gate_grad(upstream, hidden):
    sigmoid_h = jax.nn.sigmoid(hidden)
    return (upstream * sigmoid_h * (1.0 + hidden * (1.0 - sigmoid_h))).astype(jnp.bfloat16)

def reference(input_clip, cotangent, kernel_in, kernel_out):
    enc_out, enc_hidden, enc_active = section(input_clip, kernel_in[0], kernel_out[0])
    dec_out, dec_hidden, dec_active = section(enc_out, kernel_in[1], kernel_out[1])
    dec_gated = gate_grad(conv_transpose(cotangent, kernel_out[1]), dec_hidden)
    passed = (cotangent.astype(jnp.float32) + conv_transpose(dec_gated, kernel_in[1])).astype(jnp.bfloat16)
    enc_gated = gate_grad(conv_transpose(passed, kernel_out[0]), enc_hidden)
    grad_in = jnp.stack([weight_grad(input_clip, enc_gated), weight_grad(enc_out, dec_gated)])
    grad_out = jnp.stack([weight_grad(enc_active, passed), weight_grad(dec_active, cotangent)])
    return (jnp.stack([enc_out, dec_out]), grad_in, grad_out)
```

```python
from functools import partial

import jax
import jax.numpy as jnp
from jax import lax
from jax.experimental import pallas as pl
from jax.experimental.pallas import tpu as pltpu
from jax.sharding import PartitionSpec as P

BF = jnp.bfloat16
F32 = jnp.float32
NT = (((1,), (1,)), ((), ()))
TN = (((0,), (0,)), ((), ()))
VMEM_LIMIT = 56 * 1024 * 1024


class Dims:
    def __init__(self, mesh, frames_here, rows_here, width, channels, hidden):
        self.tm, self.rows = mesh["tm"], mesh["rows"]
        self.n = self.tm * self.rows
        self.f_here, self.r_here = frames_here, rows_here
        self.fr = frames_here * rows_here
        self.F, self.H = self.tm * frames_here, self.rows * rows_here
        self.W, self.C, self.D = width, channels, hidden
        self.cell = self.F * self.H
        self.own = width // self.n


def patches(v, dst, at, dims, reverse):
    F, H, c = dims.F, dims.H, v.shape[1]
    v = v.reshape(F, H, c)
    row = lax.broadcasted_iota(jnp.int32, v.shape, 1)
    for i in range(3):
        d = 1 - i if reverse else i - 1
        if d == 1:
            s = jnp.where(row == H - 1, 0.0, pltpu.roll(v, H - 1, 1))
        elif d == -1:
            s = jnp.where(row == 0, 0.0, pltpu.roll(v, 1, 1))
        else:
            s = v
        for t in range(3):
            m = 2 - t
            if m == 0:
                moved = s
            elif reverse:
                moved = jnp.concatenate([s[m:], jnp.zeros((m, H, c), F32)], axis=0)
            else:
                moved = jnp.concatenate([jnp.zeros((m, H, c), F32), s[: F - m]], axis=0)
            lane = (3 * t + i) * c
            dst[at * dims.cell : (at + 1) * dims.cell, lane : lane + c] = moved.reshape(
                F * H, c
            ).astype(BF)


def taps_of(k_ref, j, rows, axis):
    return jnp.concatenate(
        [k_ref[(3 * ti + j) * rows : (3 * ti + j + 1) * rows, :] for ti in range(9)], axis=axis
    )


def conv(p_ref, k_ref, columns, c, cell, acc_ref):
    for j in range(3):
        part = jnp.dot(
            p_ref[j * cell : (j + columns) * cell, : 9 * c],
            taps_of(k_ref, j, c, 0),
            preferred_element_type=F32,
        )
        rows = slice(0, columns * cell)
        if j == 0:
            acc_ref[rows, :] = part
        else:
            acc_ref[rows, :] += part


def conv_back(p_ref, k_ref, columns, c, c_out, cell, acc_ref):
    for j in range(3):
        part = lax.dot_general(
            p_ref[(2 - j) * cell : (2 - j + columns) * cell, : 9 * c],
            taps_of(k_ref, j, c_out, 1),
            NT,
            preferred_element_type=F32,
        )
        rows = slice(0, columns * cell)
        if j == 0:
            acc_ref[rows, :] = part
        else:
            acc_ref[rows, :] += part


def inside(meta, w, halo, dims):
    col = meta[1] * dims.own + (w - halo)
    return jnp.logical_and(col >= 0, col < dims.W)


def sigmoid(h):
    return 1.0 / (1.0 + jnp.exp(-h))


def gate(d, h):
    s = sigmoid(h)
    return d * s * (1.0 + h * (1.0 - s))


def pack_kernel(dims, meta, x_ref, g_ref, out_ref, pad, buf):
    n_cols = dims.own + 10
    pad[...] = jnp.zeros_like(pad)

    @pl.when(meta[0] == 0)
    def _():
        pad[:, 8 : 8 + dims.W, :] = x_ref[...].astype(F32)

    @pl.when(meta[0] != 0)
    def _():
        pad[:, 8 : 8 + dims.W, :] = g_ref[...].astype(F32)

    for k in range(dims.n):
        start = k * dims.own + 3
        for q in range(dims.fr):
            buf[k, q * n_cols : (q + 1) * n_cols, :] = pad[q, start : start + n_cols, :]
    out_ref[...] = buf[...].astype(BF)


def first_kernel(
    dims, meta, recv, kin_any, kout_any, slab_out, x1_out, hd_out, a_out,
    kin, kout, rbuf, slab, p1, p2, h_ref, y_ref, sems,
):
    cell, own, C, D = dims.cell, dims.own, dims.C, dims.D
    load_in = pltpu.make_async_copy(kin_any, kin, sems.at[0])
    load_out = pltpu.make_async_copy(kout_any, kout, sems.at[1])
    load_in.start()
    load_out.start()
    n_cols = own + 10
    rbuf[...] = recv[...].astype(F32)
    for s in range(dims.n):
        i, j = s // dims.rows, s % dims.rows
        for q in range(dims.fr):
            f, r = i * dims.f_here + q // dims.r_here, j * dims.r_here + q % dims.r_here
            slab[pl.ds(f * dims.H + r, n_cols, stride=cell), :] = rbuf[
                s, q * n_cols : (q + 1) * n_cols, :
            ]
    slab_out[...] = slab[4 * cell : (6 + own) * cell, :].astype(BF)

    @pl.when(meta[0] == 0)
    def _():
        for w in range(n_cols):
            patches(slab[w * cell : (w + 1) * cell, :], p1, w, dims, False)
        load_in.wait()
        conv(p1, kin, own + 8, C, cell, h_ref)
        hd_out[...] = h_ref[2 * cell : (6 + own) * cell, :]
        for w in range(own + 8):
            h = h_ref[w * cell : (w + 1) * cell, :]
            a = jnp.where(inside(meta, w, 4, dims), h * sigmoid(h), 0.0)
            if 3 <= w < 5 + own:
                a_out[(w - 3) * cell : (w - 2) * cell, :] = a.astype(BF)
            patches(a, p2, w, dims, False)
        load_out.wait()
        conv(p2, kout, own + 6, D, cell, y_ref)
        for w in range(own + 6):
            v = slab[(w + 2) * cell : (w + 3) * cell, :] + y_ref[w * cell : (w + 1) * cell, :]
            x1_out[w * cell : (w + 1) * cell, :] = jnp.where(
                inside(meta, w, 3, dims), v, 0.0
            ).astype(BF)

    @pl.when(meta[0] != 0)
    def _():
        for w in range(own + 6):
            patches(slab[(w + 2) * cell : (w + 3) * cell, :], p1, w, dims, True)
        load_in.wait()
        load_out.wait()
        conv_back(p1, kout, own + 4, C, D, cell, h_ref)
        hd_out[...] = h_ref[: (own + 4) * cell, :]
        x1_out[...] = jnp.zeros_like(x1_out)
        a_out[...] = jnp.zeros_like(a_out)


def second_kernel(
    dims, meta, x1, hd, gslab, a_in, kin_any, g0_out, a_out, e_out,
    kin, p1, p2, h_ref, y_ref, sems,
):
    cell, own, C, D = dims.cell, dims.own, dims.C, dims.D

    @pl.when(meta[0] == 0)
    def _():
        a_out[...] = a_in[...]
        g0_out[...] = jnp.zeros_like(g0_out)
        e_out[...] = jnp.zeros_like(e_out)

    @pl.when(meta[0] != 0)
    def _():
        load_in = pltpu.make_async_copy(kin_any, kin, sems.at[0])
        load_in.start()
        for w in range(own + 6):
            patches(x1[w * cell : (w + 1) * cell, :].astype(F32), p1, w, dims, False)
        load_in.wait()
        conv(p1, kin, own + 4, C, cell, h_ref)
        for w in range(own + 4):
            rows = slice(w * cell, (w + 1) * cell)
            h = h_ref[rows, :]
            if 1 <= w < 3 + own:
                a = jnp.where(inside(meta, w, 2, dims), h * sigmoid(h), 0.0)
                a_out[(w - 1) * cell : w * cell, :] = a.astype(BF)
            e = jnp.where(inside(meta, w, 2, dims), gate(hd[rows, :], h), 0.0)
            if 2 <= w < 2 + own:
                e_out[(w - 2) * cell : (w - 1) * cell, :] = e.astype(BF)
            patches(e, p2, w, dims, True)
        conv_back(p2, kin, own + 2, D, C, cell, y_ref)
        for w in range(own + 2):
            rows = slice(w * cell, (w + 1) * cell)
            v = gslab[rows, :].astype(F32) + y_ref[rows, :]
            g0_out[rows, :] = jnp.where(inside(meta, w, 1, dims), v, 0.0).astype(BF)


def third_kernel(
    dims, meta, g0, hd, x1, a_in, e_in, kout_any, e_out, sec_out,
    kout, p2, h_ref, y_ref, sems,
):
    cell, own, C, D = dims.cell, dims.own, dims.C, dims.D
    load_out = pltpu.make_async_copy(kout_any, kout, sems.at[0])
    load_out.start()

    @pl.when(meta[0] == 0)
    def _():
        for w in range(own + 2):
            patches(g0[w * cell : (w + 1) * cell, :].astype(F32), p2, w, dims, True)
        load_out.wait()
        conv_back(p2, kout, own, C, D, cell, h_ref)
        for w in range(own):
            rows = slice(w * cell, (w + 1) * cell)
            e_out[rows, :] = gate(
                h_ref[rows, :], hd[(w + 2) * cell : (w + 3) * cell, :]
            ).astype(BF)
        sec_out[...] = x1[3 * cell : (3 + own) * cell, :]

    @pl.when(meta[0] != 0)
    def _():
        for w in range(own + 2):
            patches(a_in[w * cell : (w + 1) * cell, :].astype(F32), p2, w, dims, False)
        load_out.wait()
        conv(p2, kout, own, D, cell, y_ref)
        sec_out[...] = (
            x1[3 * cell : (3 + own) * cell, :].astype(F32) + y_ref[: own * cell, :]
        ).astype(BF)
        e_out[...] = e_in[...]


def grad_kernel(dims, c, v_ref, u_ref, out_ref, p):
    cell, own = dims.cell, dims.own
    for w in range(own + 2):
        patches(v_ref[w * cell : (w + 1) * cell, :].astype(F32), p, w, dims, False)
    for j in range(3):
        g = lax.dot_general(
            p[j * cell : (j + own) * cell, :], u_ref[...], TN, preferred_element_type=F32
        )
        for ti in range(9):
            out_ref[(3 * ti + j) * c : (3 * ti + j + 1) * c, :] = g[ti * c : (ti + 1) * c, :]


def call(kernel, shapes, ins, scratch, cost, name):
    return pl.pallas_call(
        kernel,
        out_shape=shapes,
        in_specs=ins,
        out_specs=jax.tree.map(lambda _: pl.BlockSpec(memory_space=pltpu.VMEM), shapes),
        scratch_shapes=scratch,
        compiler_params=pltpu.CompilerParams(vmem_limit_bytes=VMEM_LIMIT),
        cost_estimate=pl.CostEstimate(flops=cost, bytes_accessed=4 << 20, transcendentals=0),
        name=name,
    )


def halved(parts, axis, mine, bit, dim, apart):
    count = lax.axis_size(axis)
    flag = mine == 1
    low = lax.index_in_dim(parts, 0, dim, keepdims=False)
    high = lax.index_in_dim(parts, 1, dim, keepdims=False)
    send = jnp.where(flag, low, high).astype(BF)
    keep = jnp.where(flag, high, low)
    got = lax.ppermute(send, axis, [(i, i ^ apart) for i in range(count)])
    return keep + got.astype(F32)


def reduce_scatter(parts, dims):
    m = parts.shape[0] // dims.n
    order = []
    for axis, size in (("rows", dims.rows), ("tm", dims.tm)):
        apart = 1
        while apart < size:
            order.append((axis, apart))
            apart *= 2
    tm_bits = dims.tm.bit_length() - 1
    row_bits = dims.rows.bit_length() - 1
    names = [("tm", 1 << b) for b in reversed(range(tm_bits))]
    names += [("rows", 1 << b) for b in reversed(range(row_bits))]
    parts = parts.reshape((2,) * len(names) + (m, 128))
    for axis, apart in order:
        dim = names.index((axis, apart))
        mine = (lax.axis_index(axis) // apart) % 2
        parts = halved(parts, axis, mine, None, dim, apart)
        names.pop(dim)
    return parts


def on_device(shape, input_clip, cotangent, kernel_in, kernel_out):
    f_here, r_here, W, C = input_clip.shape
    D = kernel_in.shape[2]
    dims = Dims(shape, f_here, r_here, W, C, D)
    own, cell, n = dims.own, dims.cell, dims.n
    kin, kout = kernel_in[0], kernel_out[0]
    role = lax.axis_index("segment")
    k = lax.axis_index("tm") * dims.rows + lax.axis_index("rows")
    meta = jnp.stack([role, k]).astype(jnp.int32)
    smem = pl.BlockSpec(memory_space=pltpu.SMEM)
    vm = pl.BlockSpec(memory_space=pltpu.VMEM)
    hbm = pl.BlockSpec(memory_space=pl.ANY)
    sds = jax.ShapeDtypeStruct
    n_cols = own + 10
    fr = dims.fr
    conv_flops = 2 * 27 * C * D * cell

    send = call(
        partial(pack_kernel, dims), sds((n, fr * n_cols, C), BF), [smem, vm, vm],
        [pltpu.VMEM((fr, W + 16, C), F32), pltpu.VMEM((n, fr * n_cols, C), F32)], 0, "pack",
    )(meta, input_clip.reshape(fr, W, C), cotangent.reshape(fr, W, C))
    recv = lax.all_to_all(send, ("tm", "rows"), 0, 0)

    slab, x1, hd, a0 = call(
        partial(first_kernel, dims),
        (
            sds(((own + 2) * cell, C), BF), sds(((own + 6) * cell, C), BF),
            sds(((own + 4) * cell, D), F32), sds(((own + 2) * cell, D), BF),
        ),
        [smem, vm, hbm, hbm],
        [
            pltpu.VMEM(kin.shape, BF), pltpu.VMEM(kout.shape, BF),
            pltpu.VMEM((n, fr * n_cols, C), F32), pltpu.VMEM((n_cols * cell, C), F32),
            pltpu.VMEM((n_cols * cell, 9 * C), BF), pltpu.VMEM(((own + 8) * cell, 9 * D), BF),
            pltpu.VMEM(((own + 8) * cell, D), F32), pltpu.VMEM(((own + 6) * cell, C), F32),
            pltpu.SemaphoreType.DMA((2,)),
        ],
        conv_flops * 2 * (own + 7), "first",
    )(meta, recv, kin, kout)

    swap = [(0, 1), (1, 0)]
    x1_there = lax.ppermute(x1, "segment", swap)

    g0_here, a, e1 = call(
        partial(second_kernel, dims),
        (
            sds(((own + 2) * cell, C), BF), sds(((own + 2) * cell, D), BF),
            sds((own * cell, D), BF),
        ),
        [smem, vm, vm, vm, vm, hbm],
        [
            pltpu.VMEM(kin.shape, BF),
            pltpu.VMEM(((own + 6) * cell, 9 * C), BF), pltpu.VMEM(((own + 4) * cell, 9 * D), BF),
            pltpu.VMEM(((own + 4) * cell, D), F32), pltpu.VMEM(((own + 2) * cell, C), F32),
            pltpu.SemaphoreType.DMA((1,)),
        ],
        conv_flops * 2 * (own + 3), "second",
    )(meta, x1_there, hd, slab, a0, kin)

    g0_there = lax.ppermute(g0_here, "segment", swap)
    on_encoder = role == 0
    x_here = jnp.where(on_encoder, x1, x1_there)

    e, sec = call(
        partial(third_kernel, dims),
        (sds((own * cell, D), BF), sds((own * cell, C), BF)),
        [smem, vm, vm, vm, vm, vm, hbm],
        [
            pltpu.VMEM(kout.shape, BF), pltpu.VMEM(((own + 2) * cell, 9 * D), BF),
            pltpu.VMEM((own * cell, D), F32), pltpu.VMEM((own * cell, C), F32),
            pltpu.SemaphoreType.DMA((1,)),
        ],
        conv_flops * own, "third",
    )(meta, g0_there, hd, x_here, a, e1, kout)

    g = jnp.where(on_encoder, g0_there, slab)[cell : (1 + own) * cell]
    x = jnp.where(on_encoder, slab, x1_there[2 * cell : (4 + own) * cell])

    def grad(c, c_out, v, u, name):
        return call(
            partial(grad_kernel, dims, c), sds((27 * c, c_out), F32), [vm, vm],
            [pltpu.VMEM(((own + 2) * cell, 9 * c), BF)], conv_flops * own, name,
        )(v, u)

    out_part = grad(D, C, a, g, "grad_out")
    in_part = grad(C, D, x, e, "grad_in")
    out_sum = reduce_scatter(out_part.reshape(-1, 128), dims).reshape(-1)
    in_sum = reduce_scatter(in_part.reshape(-1, 128), dims).reshape(-1)

    back = sec.reshape(own, dims.tm, f_here, dims.rows, r_here, C)
    back = back.transpose(1, 3, 2, 4, 0, 5).reshape(n, fr * own, C)
    back = lax.all_to_all(back, ("tm", "rows"), 0, 0)
    sections = back.reshape(n, fr, own, C).transpose(1, 0, 2, 3).reshape(f_here, r_here, W, C)
    return sections[None], in_sum[None], out_sum[None]


def solution(mesh):
    in_specs = (
        P("tm", "rows", None, None),
        P("tm", "rows", None, None),
        P("segment", None, None),
        P("segment", None, None),
    )
    out_specs = (
        P("segment", "tm", "rows", None, None),
        P("segment", ("tm", "rows")),
        P("segment", ("tm", "rows")),
    )
    return jax.shard_map(
        partial(on_device, dict(mesh.shape)), mesh=mesh, in_specs=in_specs,
        out_specs=out_specs, check_vma=False,
    )
```

```python
from functools import partial

import jax
import jax.numpy as jnp
from jax import lax
from jax.experimental import pallas as pl
from jax.experimental.pallas import tpu as pltpu
from jax.sharding import PartitionSpec as P

BF = jnp.bfloat16
F32 = jnp.float32
NT = (((1,), (1,)), ((), ()))
LANES = 128
IN_GATHER = ("rows", 2)
OUT_GATHER = ("tm", 1)
IN_ORDER = (("tm", 1), ("tm", 2))
OUT_ORDER = (("rows", 2), ("tm", 2))


class Dims:
    def __init__(self, mesh, frames_here, rows_here, width, channels, hidden):
        self.tm, self.rows = mesh["tm"], mesh["rows"]
        self.n = self.tm * self.rows
        self.f_here, self.r_here = frames_here, rows_here
        self.fr = frames_here * rows_here
        self.F, self.H = self.tm * frames_here, self.rows * rows_here
        self.W, self.C, self.D = width, channels, hidden
        self.cell = self.F * self.H
        self.own = width // self.n
        self.vmem = (24 << 20) if self.cell <= 64 else (56 << 20)

    def slab_of(self, device):
        i, j = device // self.rows, device % self.rows
        return i * self.rows + (j if i % 2 == 0 else self.rows - 1 - j)

    def my_role(self):
        return lax.axis_index("segment")

    def my_device(self):
        return lax.axis_index("tm") * self.rows + lax.axis_index("rows")

    def my_slab(self):
        i, j = lax.axis_index("tm"), lax.axis_index("rows")
        return i * self.rows + jnp.where(lax.rem(i, 2) == 0, j, self.rows - 1 - j)

    def edge(self, halo):
        columns = min(self.own, halo)
        return columns, halo // columns


def sides_of(v, dims):
    v = v.reshape(dims.F, dims.H, v.shape[1])
    row = lax.broadcasted_iota(jnp.int32, v.shape, 1)
    before = jnp.where(row == 0, 0.0, pltpu.roll(v, 1, 1))
    after = jnp.where(row == dims.H - 1, 0.0, pltpu.roll(v, dims.H - 1, 1))
    return before, v, after


def patches(v, dst, at, dims, reverse):
    F, H, c = dims.F, dims.H, v.shape[1]
    sides = sides_of(v, dims)
    for i in range(3):
        s = sides[2 - i] if reverse else sides[i]
        for t in range(3):
            m = 2 - t
            if m == 0:
                moved = s
            elif reverse:
                moved = jnp.concatenate([s[m:], jnp.zeros((m, H, c), F32)], axis=0)
            else:
                moved = jnp.concatenate([jnp.zeros((m, H, c), F32), s[: F - m]], axis=0)
            lane = (3 * t + i) * c
            dst[at * dims.cell : (at + 1) * dims.cell, lane : lane + c] = moved.reshape(
                F * H, c
            ).astype(BF)


def taps_of(k_ref, j, rows, axis):
    return jnp.concatenate(
        [k_ref[(3 * ti + j) * rows : (3 * ti + j + 1) * rows, :] for ti in range(9)], axis=axis
    )


def conv(p_ref, k_ref, columns, c, cell, acc_ref):
    for j in range(3):
        part = jnp.dot(
            p_ref[j * cell : (j + columns) * cell, :],
            taps_of(k_ref, j, c, 0),
            preferred_element_type=F32,
        )
        if j == 0:
            acc_ref[...] = part
        else:
            acc_ref[...] += part


def conv_back(p_ref, k_ref, columns, c_out, cell, acc_ref):
    for j in range(3):
        part = lax.dot_general(
            p_ref[(2 - j) * cell : (2 - j + columns) * cell, :],
            taps_of(k_ref, j, c_out, 1),
            NT,
            preferred_element_type=F32,
        )
        if j == 0:
            acc_ref[...] = part
        else:
            acc_ref[...] += part


def sigmoid(h):
    return 1.0 / (1.0 + jnp.exp(-h))


def gate(d, h):
    s = sigmoid(h)
    return d * s * (1.0 + h * (1.0 - s))


def column(w, dims):
    return slice(w * dims.cell, (w + 1) * dims.cell)


def within(w, halo, slab, dims):
    at = slab * dims.own + (w - halo)
    return jnp.logical_and(at >= 0, at < dims.W)


def load(pairs, sems):
    copies = [pltpu.make_async_copy(src, dst, sems.at[at]) for at, (src, dst) in enumerate(pairs)]
    for copy in copies:
        copy.start()
    return copies


def store_hidden(dst, w, a, dims):
    a = a.astype(BF)
    for h in range(dims.D // LANES):
        dst[column(h * (dims.own + 2) + w, dims), :] = a[:, h * LANES : (h + 1) * LANES]


def hidden_column(src, w, dims):
    parts = [src[column(h * (dims.own + 2) + w, dims), :] for h in range(dims.D // LANES)]
    return jnp.concatenate([part.astype(F32) for part in parts], axis=1)


def pack_kernel(dims, z_ref, out_ref, pad, buf):
    cols = dims.own + 6
    pad[:, :8, :] = jnp.zeros((dims.fr, 8, dims.C), F32)
    pad[:, 8 + dims.W :, :] = jnp.zeros((dims.fr, 8, dims.C), F32)
    pad[:, 8 : 8 + dims.W, :] = z_ref[...].astype(F32)
    for d in range(dims.n):
        start = dims.slab_of(d) * dims.own + 5
        for q in range(dims.fr):
            at = (d * dims.fr + q) * cols
            buf[at : at + cols, :] = pad[q, start : start + cols, :]
    out_ref[...] = buf[...].astype(BF)


def first_kernel(
    dims, recv_hbm, kin_hbm, kout_hbm, z_out, a_out, x1_out, lo_out, hi_out, hd_out,
    recv, kin, kout, rbuf, slab, p1, p2, y_ref, sems,
):
    cell, own, C, D = dims.cell, dims.own, dims.C, dims.D
    load_recv, load_in, load_out = load(
        [(recv_hbm, recv), (kin_hbm, kin), (kout_hbm, kout)], sems
    )
    cols = own + 6
    role, k = dims.my_role(), dims.my_slab()
    load_recv.wait()
    rbuf[...] = recv[...].astype(F32)
    for s in range(dims.n):
        i, j = s // dims.rows, s % dims.rows
        for q in range(dims.fr):
            f, r = i * dims.f_here + q // dims.r_here, j * dims.r_here + q % dims.r_here
            at = (s * dims.fr + q) * cols
            slab[pl.ds(f * dims.H + r, cols, stride=cell), :] = rbuf[at : at + cols, :]
    z_out[...] = slab[2 * cell : (4 + own) * cell, :].astype(BF)

    @pl.when(role == 0)
    def _():
        for w in range(own + 4):
            patches(slab[column(w + 1, dims), :], p1, w, dims, False)
        load_in.wait()
        mine = slice(cell, (3 + own) * cell)
        conv(p1, kin, own + 2, C, cell, hd_out.at[mine])
        for w in range(own + 2):
            h = hd_out[column(w + 1, dims), :]
            a = jnp.where(within(w, 1, k, dims), h * sigmoid(h), 0.0)
            store_hidden(a_out, w, a, dims)
            patches(a, p2, w, dims, False)
        load_out.wait()
        conv(p2, kout, own, D, cell, y_ref)
        x1_out[...] = (slab[3 * cell : (3 + own) * cell, :] + y_ref[...]).astype(BF)
        e_rows = lo_out.shape[0]
        lo_out[...] = x1_out[:e_rows, :]
        hi_out[...] = x1_out[own * cell - e_rows :, :]

    @pl.when(role != 0)
    def _():
        for w in range(cols):
            patches(slab[column(w, dims), :], p1, w, dims, True)
        load_in.wait()
        load_out.wait()
        conv_back(p1, kout, own + 4, D, cell, hd_out)


def second_kernel(dims, n_edge, *refs):
    edges = 2 * n_edge + 1
    x_hbm = refs[:edges]
    hd_hbm, z_hbm, a_hbm, kin_hbm = refs[edges : edges + 4]
    g0_out, x_out, a_out, e_out = refs[edges + 4 : edges + 8]
    kin, x1, hd, z, p1, p2, h_ref, y_ref, sems = refs[edges + 8 :]
    cell, own, C, D = dims.cell, dims.own, dims.C, dims.D
    role, k = dims.my_role(), dims.my_slab()

    @pl.when(role == 0)
    def _():
        for copy in load([(z_hbm, x_out), (a_hbm, a_out)], sems):
            copy.wait()

    @pl.when(role != 0)
    def _():
        pairs, at = [], 0
        for ref in x_hbm:
            rows = ref.shape[0]
            pairs.append((ref, x1.at[pl.ds(at, rows), :]))
            at += rows
        copies = load(pairs + [(kin_hbm, kin), (hd_hbm, hd), (z_hbm, z)], sems)
        for copy in copies[:edges]:
            copy.wait()
        x_out[...] = x1[2 * cell : (4 + own) * cell, :]
        for w in range(own + 6):
            patches(x1[column(w, dims), :].astype(F32), p1, w, dims, False)
        for copy in copies[edges:]:
            copy.wait()
        conv(p1, kin, own + 4, C, cell, h_ref)
        for w in range(own + 4):
            h = h_ref[column(w, dims), :]
            ok = within(w, 2, k, dims)
            s = sigmoid(h)
            if 1 <= w < 3 + own:
                store_hidden(a_out, w - 1, jnp.where(ok, h * s, 0.0), dims)
            e = hd[column(w, dims), :] * s * (1.0 + h * (1.0 - s))
            e = jnp.where(ok, e, 0.0)
            if 2 <= w < 2 + own:
                e_out[column(w - 2, dims), :] = e.astype(BF)
            patches(e, p2, w, dims, True)
        conv_back(p2, kin, own + 2, C, cell, y_ref)
        for w in range(own + 2):
            v = z[column(w, dims), :].astype(F32) + y_ref[column(w, dims), :]
            g0_out[column(w, dims), :] = jnp.where(within(w, 1, k, dims), v, 0.0).astype(BF)


def third_kernel(
    dims, g0_hbm, hd_hbm, x1_hbm, z_hbm, x_hbm, a_hbm, e_hbm, kout_hbm, e_out, g_out, sec_out,
    g0, hd, x1, z, x, a, kout, p1, p2, h_ref, y_ref, buf, sems,
):
    cell, own, C, D = dims.cell, dims.own, dims.C, dims.D
    role = dims.my_role()
    cols = own + 2
    mine = slice(cell, (1 + own) * cell)

    @pl.when(role == 0)
    def _():
        load_g, load_k, load_h, load_x = load(
            [(g0_hbm, g0), (kout_hbm, kout), (hd_hbm, hd), (x1_hbm, x1)], sems
        )
        load_g.wait()
        g_out[...] = g0[mine, :]
        for w in range(cols):
            patches(g0[column(w, dims), :].astype(F32), p1, w, dims, True)
        load_k.wait()
        conv_back(p1, kout, own, D, cell, h_ref)
        load_h.wait()
        for w in range(own):
            e_out[column(w, dims), :] = gate(
                h_ref[column(w, dims), :], hd[column(w + 2, dims), :]
            ).astype(BF)
        load_x.wait()
        y_ref[...] = x1[...].astype(F32)

    @pl.when(role != 0)
    def _():
        load_a, load_k, load_x, load_g, load_e = load(
            [(a_hbm, a), (kout_hbm, kout), (x_hbm, x), (z_hbm, z), (e_hbm, e_out)], sems
        )
        load_a.wait()
        for w in range(cols):
            patches(hidden_column(a, w, dims), p2, w, dims, False)
        load_k.wait()
        conv(p2, kout, own, D, cell, y_ref)
        load_x.wait()
        y_ref[...] = y_ref[...] + x[mine, :].astype(F32)
        load_g.wait()
        g_out[...] = z[mine, :]
        load_e.wait()

    for d in range(dims.n):
        i, j = d // dims.rows, d % dims.rows
        for q in range(dims.fr):
            f, r = i * dims.f_here + q // dims.r_here, j * dims.r_here + q % dims.r_here
            at = (d * dims.fr + q) * own
            buf[at : at + own, :] = y_ref[pl.ds(f * dims.H + r, own, stride=cell), :]
    sec_out[...] = buf[...].astype(BF)


def unpack_kernel(dims, recv, out_ref, rbuf, buf):
    own = dims.own
    rbuf[...] = recv[...].astype(F32)
    for d in range(dims.n):
        at = dims.slab_of(d) * own
        for q in range(dims.fr):
            src = (d * dims.fr + q) * own
            buf[q, at : at + own, :] = rbuf[src : src + own, :]
    out_ref[...] = buf[...].astype(BF)


def chunk_of(dims, c):
    rows = 27 * c // dims.n
    return rows, -(-rows // 16) * 16


def grads_kernel(
    dims, in_masks, out_masks,
    x_mine, x_beside, a_mine, a_beside, e_mine, e_beside, g_mine, g_beside, keep, send,
    x, a, e, g, p_in, p_out, ut_in, ut_out, win_in, win_out, sems,
):
    cell, own, C, D = dims.cell, dims.own, dims.C, dims.D
    cols = own + 2
    copies = load(
        [
            (a_mine, a.at[0]), (a_beside, a.at[1]), (g_mine, g.at[0]), (g_beside, g.at[1]),
            (x_mine, x.at[0]), (x_beside, x.at[1]), (e_mine, e.at[0]), (e_beside, e.at[1]),
        ],
        sems,
    )

    def sums(c, p, column_of, u, ut, waits, win):
        for s in range(2):
            waits[s].wait()
            for w in range(cols):
                patches(column_of(s, w), p, s * cols + w, dims, False)
        for s in range(2):
            waits[2 + s].wait()
            ut[:, s * own * cell : (s + 1) * own * cell] = u[s].T
        for j in range(3):
            cells = [p[(s * cols + j) * cell : (s * cols + j + own) * cell, :] for s in range(2)]
            part = jnp.dot(ut[...], jnp.concatenate(cells, axis=0), preferred_element_type=F32)
            for ti in range(9):
                at = 3 * ti + j
                win[at * c : (at + 1) * c, :] = part[:, ti * c : (ti + 1) * c].T

    sums(D, p_out, lambda s, w: hidden_column(a.at[s], w, dims), g, ut_out, copies[:4], win_out)
    sums(
        C, p_in, lambda s, w: x[s, column(w, dims), :].astype(F32), e, ut_in, copies[4:], win_in
    )
    me = dims.my_device()

    def rows_of(win, mask, length):
        start = lax.bitwise_xor(me, mask) * length
        if length % 8 == 0:
            return win[pl.ds(pl.multiple_of(start, 8), length), :]
        size = -(-(length + 7) // 8) * 8
        base = lax.div(start, 8) * 8
        rows = win[pl.ds(pl.multiple_of(base, 8), size), :]
        return pltpu.roll(rows, size - (start - base), 0)[:length]

    length_in, padded_in = chunk_of(dims, C)
    length_out, padded_out = chunk_of(dims, D)
    for at, (in_mask, out_mask) in enumerate(zip(in_masks, out_masks)):
        pieces = [(0, rows_of(win_out, out_mask, length_out))]
        rows = rows_of(win_in, in_mask, length_in)
        for h in range(D // LANES):
            pieces.append((padded_out + h * padded_in, rows[:, h * LANES : (h + 1) * LANES]))
        for first, piece in pieces:
            if at % 2 == 0:
                keep[at // 2, first : first + piece.shape[0], :] = piece
            else:
                send[at // 2, first : first + piece.shape[0], :] = piece.astype(BF)


def split_kernel(padded_out, keep, got, out_keep, out_send, in_keep, in_send):
    for at in range(keep.shape[0]):
        v = keep[at] + got[at].astype(F32)
        for dst, sent, part in (
            (out_keep, out_send, v[:padded_out]), (in_keep, in_send, v[padded_out:])
        ):
            if at % 2 == 0:
                dst[at // 2] = part
            else:
                sent[at // 2] = part.astype(BF)


def final_kernel(dims, in_keep, in_got, out_keep, out_got, in_out, out_out):
    length, padded = chunk_of(dims, dims.C)
    halves = dims.D // LANES
    for h in range(halves):
        rows = slice(h * padded, h * padded + length)
        in_out[pl.ds(h, length, stride=halves), :] = in_keep[rows, :] + in_got[rows, :].astype(F32)
    length = out_out.shape[0]
    out_out[...] = out_keep[:length, :] + out_got[:length, :].astype(F32)


def call(dims, kernel, shapes, ins, scratch, cost, name, vmem=None):
    return pl.pallas_call(
        kernel,
        out_shape=shapes,
        in_specs=ins,
        out_specs=jax.tree.map(lambda _: pl.BlockSpec(memory_space=pltpu.VMEM), shapes),
        scratch_shapes=scratch,
        compiler_params=pltpu.CompilerParams(vmem_limit_bytes=vmem or dims.vmem),
        cost_estimate=pl.CostEstimate(flops=cost, bytes_accessed=4 << 20, transcendentals=0),
        name=name,
    )


def halving_steps(dims, order):
    steps = [("rows", 1)] + list(order)
    for axis, size in (("tm", dims.tm), ("rows", dims.rows)):
        apart = 4
        while apart < size:
            steps.append((axis, apart))
            apart *= 2
    steps = [(axis, apart, apart * (dims.rows if axis == "tm" else 1)) for axis, apart in steps]
    masks = [sum(s[2] for b, s in enumerate(steps) if m >> b & 1) for m in range(1 << len(steps))]
    return steps, masks


def group_swap(block, axis, apart):
    count = lax.axis_size(axis)
    return lax.ppermute(block, axis, [(i, i ^ apart) for i in range(count)])


def exchanged(blocks, n):
    got = lax.all_to_all(blocks.reshape(n, -1, blocks.shape[1]), ("tm", "rows"), 0, 0)
    return got.reshape(blocks.shape)


def edge_swap(dims, block, distance):
    pairs = []
    for k in range(dims.n):
        if 0 <= k + distance < dims.n:
            a, b = dims.slab_of(k), dims.n + dims.slab_of(k + distance)
            pairs += [(a, b), (b, a)]
    return lax.ppermute(block, ("segment", "tm", "rows"), pairs)


def added(keep, send, step):
    keep = keep + group_swap(send, step[0], step[1]).astype(F32)
    return keep[0::2], keep[1::2].astype(BF)


def on_device(shape, input_clip, cotangent, kernel_in, kernel_out):
    f_here, r_here, W, C = input_clip.shape
    D = kernel_in.shape[2]
    dims = Dims(shape, f_here, r_here, W, C, D)
    own, cell, n, fr = dims.own, dims.cell, dims.n, dims.fr
    kin, kout = (
        pltpu.with_memory_space_constraint(k, pltpu.HBM) for k in (kernel_in[0], kernel_out[0])
    )
    vm = pl.BlockSpec(memory_space=pltpu.VMEM)
    hbm = pl.BlockSpec(memory_space=pltpu.HBM)
    sds = jax.ShapeDtypeStruct
    scr = pltpu.VMEM
    cols = own + 6
    conv_flops = 2 * 27 * C * D * cell
    e_cols, e_far = dims.edge(3)
    x_shape = sds(((own + 2) * cell, C), BF)
    a_shape = sds(((own + 2) * cell * (D // LANES), LANES), BF)

    send = call(
        dims, partial(pack_kernel, dims), sds((n * fr * cols, C), BF), [vm],
        [scr((fr, W + 16, C), F32), scr((n * fr * cols, C), F32)], 0, "pack",
    )(jnp.where(dims.my_role() == 0, input_clip, cotangent).reshape(fr, W, C))
    recv = exchanged(send, n)

    z, a1, x1, x1_lo, x1_hi, hd = call(
        dims, partial(first_kernel, dims),
        (
            x_shape, a_shape, sds((own * cell, C), BF), sds((e_cols * cell, C), BF),
            sds((e_cols * cell, C), BF), sds(((own + 4) * cell, D), F32),
        ),
        [hbm] * 3,
        [
            scr((n * fr * cols, C), BF), scr(kin.shape, BF), scr(kout.shape, BF),
            scr((n * fr * cols, C), F32), scr((cols * cell, C), F32),
            scr((cols * cell, 9 * C), BF), scr(((own + 2) * cell, 9 * D), BF),
            scr((own * cell, C), F32), pltpu.SemaphoreType.DMA((3,)),
        ],
        conv_flops * 2 * (own + 2), "first",
    )(recv, kin, kout)

    x1_there = group_swap(x1, "segment", 1)
    lefts = [edge_swap(dims, x1_hi, far) for far in range(e_far, 0, -1)]
    rights = [edge_swap(dims, x1_lo, -far) for far in range(1, e_far + 1)]

    g0, x2, a2, e1 = call(
        dims, partial(second_kernel, dims, e_far),
        (x_shape, x_shape, a_shape, sds((own * cell, D), BF)),
        [hbm] * (5 + 2 * e_far),
        [
            scr(kin.shape, BF), scr((cols * cell, C), BF),
            scr(((own + 4) * cell, D), F32), scr(x_shape.shape, BF),
            scr((cols * cell, 9 * C), BF), scr(((own + 4) * cell, 9 * D), BF),
            scr(((own + 4) * cell, D), F32), scr(((own + 2) * cell, C), F32),
            pltpu.SemaphoreType.DMA((4 + 2 * e_far,)),
        ],
        conv_flops * 2 * (own + 2), "second",
    )(*lefts, x1_there, *rights, hd, z, a1, kin)

    g0_there = group_swap(g0, "segment", 1)
    a_beside = group_swap(a2, *OUT_GATHER)
    x_beside = group_swap(x2, *IN_GATHER)
    g0_there, x_beside = lax.optimization_barrier((g0_there, x_beside))

    e, g, sec = call(
        dims, partial(third_kernel, dims),
        (sds((own * cell, D), BF), sds((own * cell, C), BF), sds((n * fr * own, C), BF)),
        [hbm] * 8,
        [
            scr(g0.shape, BF), scr(hd.shape, F32), scr(x1.shape, BF),
            scr(x_shape.shape, BF), scr(x_shape.shape, BF), scr(a_shape.shape, BF),
            scr(kout.shape, BF),
            scr(((own + 2) * cell, 9 * C), BF), scr(((own + 2) * cell, 9 * D), BF),
            scr((own * cell, D), F32), scr((own * cell, C), F32),
            scr((n * fr * own, C), F32), pltpu.SemaphoreType.DMA((5,)),
        ],
        conv_flops * own, "third",
    )(g0_there, hd, x1, z, x2, a2, e1, kout)
    e_beside = group_swap(e, *IN_GATHER)
    g_beside = group_swap(g, *OUT_GATHER)
    back = exchanged(sec, n)
    e_beside, g_beside, back = lax.optimization_barrier((e_beside, g_beside, back))

    in_steps, in_masks = halving_steps(dims, IN_ORDER)
    out_steps, out_masks = halving_steps(dims, OUT_ORDER)
    half = len(in_masks) // 2
    padded_in, padded_out = chunk_of(dims, C)[1], chunk_of(dims, D)[1]
    both = padded_out + padded_in * (D // LANES)
    cells2 = 2 * (own + 2) * cell
    keep, sent = call(
        dims, partial(grads_kernel, dims, in_masks, out_masks),
        (sds((half, both, LANES), F32), sds((half, both, LANES), BF)),
        [hbm] * 8,
        [
            scr((2,) + x_shape.shape, BF), scr((2,) + a_shape.shape, BF),
            scr((2, own * cell, D), BF), scr((2, own * cell, C), BF),
            scr((cells2, 9 * C), BF), scr((cells2, 9 * D), BF),
            scr((D, 2 * own * cell), BF), scr((C, 2 * own * cell), BF),
            scr((27 * C + 64, D), F32), scr((27 * D + 64, C), F32),
            pltpu.SemaphoreType.DMA((8,)),
        ],
        2 * conv_flops * own, "grads", max(dims.vmem, 32 << 20),
    )(x2, x_beside, a2, a_beside, e, e_beside, g, g_beside)
    got = group_swap(sent, "rows", 1)
    quarter = half // 2
    out_keep, out_send, in_keep, in_send = call(
        dims, partial(split_kernel, padded_out),
        (
            sds((quarter, padded_out, LANES), F32), sds((quarter, padded_out, LANES), BF),
            sds((quarter, both - padded_out, LANES), F32),
            sds((quarter, both - padded_out, LANES), BF),
        ),
        [vm, vm], [], 0, "split",
    )(keep, got)
    for out_step, in_step in zip(out_steps[1:-1], in_steps[1:-1]):
        out_keep, out_send = added(out_keep, out_send, out_step)
        in_keep, in_send = added(in_keep, in_send, in_step)
    out_got = group_swap(out_send[0], *out_steps[-1][:2])
    in_got = group_swap(in_send[0], *in_steps[-1][:2])
    shard = 27 * C * D // n // LANES
    in_sum, out_sum = call(
        dims, partial(final_kernel, dims), (sds((shard, LANES), F32),) * 2, [vm] * 4, [], 0, "final",
    )(in_keep[0], in_got, out_keep[0], out_got)

    sections = call(
        dims, partial(unpack_kernel, dims), sds((fr, W, C), BF), [vm],
        [scr((n * fr * own, C), F32), scr((fr, W, C), F32)], 0, "unpack",
    )(back).reshape(f_here, r_here, W, C)
    return sections[None], in_sum.reshape(1, -1), out_sum.reshape(1, -1)


def solution(mesh):
    in_specs = (
        P("tm", "rows", None, None),
        P("tm", "rows", None, None),
        P("segment", None, None),
        P("segment", None, None),
    )
    out_specs = (
        P("segment", "tm", "rows", None, None),
        P("segment", ("tm", "rows")),
        P("segment", ("tm", "rows")),
    )
    return jax.shard_map(
        partial(on_device, dict(mesh.shape)), mesh=mesh, in_specs=in_specs,
        out_specs=out_specs, check_vma=False,
    )
```

```python
from functools import partial

import jax
import jax.numpy as jnp
from jax import lax
from jax.experimental import pallas as pl
from jax.experimental.pallas import tpu as pltpu
from jax.sharding import PartitionSpec as P

BF = jnp.bfloat16
F32 = jnp.float32
NT = (((1,), (1,)), ((), ()))
LANES = 128
IN_GATHER = ("rows", 2)
OUT_GATHER = ("tm", 1)
IN_ORDER = (("tm", 1), ("tm", 2))
OUT_ORDER = (("rows", 2), ("tm", 2))


class Dims:
    def __init__(self, mesh, frames_here, rows_here, width, channels, hidden):
        self.tm, self.rows = mesh["tm"], mesh["rows"]
        self.n = self.tm * self.rows
        self.f_here, self.r_here = frames_here, rows_here
        self.fr = frames_here * rows_here
        self.F, self.H = self.tm * frames_here, self.rows * rows_here
        self.W, self.C, self.D = width, channels, hidden
        self.cell = self.F * self.H
        self.own = width // self.n
        self.vmem = (24 << 20) if self.cell <= 64 else (56 << 20)

    def slab_of(self, device):
        i, j = device // self.rows, device % self.rows
        return i * self.rows + (j if i % 2 == 0 else self.rows - 1 - j)

    def my_role(self):
        return lax.axis_index("segment")

    def my_device(self):
        return lax.axis_index("tm") * self.rows + lax.axis_index("rows")

    def my_slab(self):
        i, j = lax.axis_index("tm"), lax.axis_index("rows")
        return i * self.rows + jnp.where(lax.rem(i, 2) == 0, j, self.rows - 1 - j)

    def edge(self, halo):
        columns = min(self.own, halo)
        return columns, halo // columns


def sides_of(v, dims):
    v = v.reshape(dims.F, dims.H, v.shape[1])
    row = lax.broadcasted_iota(jnp.int32, v.shape, 1)
    before = jnp.where(row == 0, 0.0, pltpu.roll(v, 1, 1))
    after = jnp.where(row == dims.H - 1, 0.0, pltpu.roll(v, dims.H - 1, 1))
    return before, v, after


def patches(v, dst, at, dims, reverse):
    F, H, c = dims.F, dims.H, v.shape[1]
    sides = sides_of(v, dims)
    cell = dims.cell
    for i in range(3):
        s = sides[2 - i] if reverse else sides[i]
        whole = s.reshape(cell, c).astype(BF)
        for t in range(3):
            m = (2 - t) * H
            if m == 0:
                moved = whole
            elif m % 16 == 0:
                gap = jnp.zeros((m, c), BF)
                parts = [whole[m:], gap] if reverse else [gap, whole[: cell - m]]
                moved = jnp.concatenate(parts, axis=0)
            else:
                gap, flat = jnp.zeros((m, c), F32), s.reshape(cell, c)
                parts = [flat[m:], gap] if reverse else [gap, flat[: cell - m]]
                moved = jnp.concatenate(parts, axis=0).astype(BF)
            lane = (3 * t + i) * c
            dst[at * cell : (at + 1) * cell, lane : lane + c] = moved


def taps_of(k_ref, j, rows, axis):
    return jnp.concatenate(
        [k_ref[(3 * ti + j) * rows : (3 * ti + j + 1) * rows, :] for ti in range(9)], axis=axis
    )


def conv(p_ref, k_ref, columns, c, cell, acc_ref):
    for j in range(3):
        part = jnp.dot(
            p_ref[j * cell : (j + columns) * cell, :],
            taps_of(k_ref, j, c, 0),
            preferred_element_type=F32,
        )
        if j == 0:
            acc_ref[...] = part
        else:
            acc_ref[...] += part


def conv_block(p_ref, k_ref, first, columns, c, cell):
    total = None
    for j in range(3):
        part = jnp.dot(
            p_ref[(first + j) * cell : (first + j + columns) * cell, :],
            taps_of(k_ref, j, c, 0),
            preferred_element_type=F32,
        )
        total = part if total is None else total + part
    return total


def blocks_of(columns, count):
    size = -(-columns // count)
    return [(at, min(size, columns - at)) for at in range(0, columns, size)]


def blocks_after(columns, earlier):
    head = earlier[0][1] - 2
    if len(earlier) < 2 or head < 1 or head >= columns:
        return [(0, columns)]
    return [(0, head), (head, columns - head)]


def conv_back_block(p_ref, k_ref, first, columns, c_out, cell):
    total = None
    for j in range(3):
        part = lax.dot_general(
            p_ref[(first + 2 - j) * cell : (first + 2 - j + columns) * cell, :],
            taps_of(k_ref, j, c_out, 1),
            NT,
            preferred_element_type=F32,
        )
        total = part if total is None else total + part
    return total


def conv_back(p_ref, k_ref, columns, c_out, cell, acc_ref):
    for j in range(3):
        part = lax.dot_general(
            p_ref[(2 - j) * cell : (2 - j + columns) * cell, :],
            taps_of(k_ref, j, c_out, 1),
            NT,
            preferred_element_type=F32,
        )
        if j == 0:
            acc_ref[...] = part
        else:
            acc_ref[...] += part


def sigmoid(h):
    return 1.0 / (1.0 + jnp.exp(-h))


def gate(d, h):
    s = sigmoid(h)
    return d * s * (1.0 + h * (1.0 - s))


def column(w, dims):
    return slice(w * dims.cell, (w + 1) * dims.cell)


def within(w, halo, slab, dims):
    at = slab * dims.own + (w - halo)
    return jnp.logical_and(at >= 0, at < dims.W)


def load(pairs, sems):
    copies = [pltpu.make_async_copy(src, dst, sems.at[at]) for at, (src, dst) in enumerate(pairs)]
    for copy in copies:
        copy.start()
    return copies


def store_hidden(dst, w, a, dims):
    a = a.astype(BF)
    for h in range(dims.D // LANES):
        dst[column(h * (dims.own + 2) + w, dims), :] = a[:, h * LANES : (h + 1) * LANES]


def hidden_column(src, w, dims):
    parts = [src[column(h * (dims.own + 2) + w, dims), :] for h in range(dims.D // LANES)]
    return jnp.concatenate([part.astype(F32) for part in parts], axis=1)


def pack_kernel(dims, z_ref, out_ref, pad, buf):
    cols = dims.own + 6
    pad[:, :8, :] = jnp.zeros((dims.fr, 8, dims.C), F32)
    pad[:, 8 + dims.W :, :] = jnp.zeros((dims.fr, 8, dims.C), F32)
    pad[:, 8 : 8 + dims.W, :] = z_ref[...].astype(F32)
    for d in range(dims.n):
        start = dims.slab_of(d) * dims.own + 5
        for q in range(dims.fr):
            at = (d * dims.fr + q) * cols
            buf[at : at + cols, :] = pad[q, start : start + cols, :]
    out_ref[...] = buf[...].astype(BF)


def first_kernel(
    dims, recv_hbm, kin_hbm, kout_hbm, z_out, a_out, x1_out, lo_out, hi_out, hd_out,
    recv, kin, kout, rbuf, slab, p1, p2, y_ref, sems,
):
    cell, own, C, D = dims.cell, dims.own, dims.C, dims.D
    load_recv, load_in, load_out = load(
        [(recv_hbm, recv), (kin_hbm, kin), (kout_hbm, kout)], sems
    )
    cols = own + 6
    role, k = dims.my_role(), dims.my_slab()
    load_recv.wait()
    rbuf[...] = recv[...].astype(F32)
    for s in range(dims.n):
        i, j = s // dims.rows, s % dims.rows
        for q in range(dims.fr):
            f, r = i * dims.f_here + q // dims.r_here, j * dims.r_here + q % dims.r_here
            at = (s * dims.fr + q) * cols
            slab[pl.ds(f * dims.H + r, cols, stride=cell), :] = rbuf[at : at + cols, :]
    z_out[...] = slab[2 * cell : (4 + own) * cell, :].astype(BF)

    @pl.when(role == 0)
    def _():
        for w in range(own + 4):
            patches(slab[column(w + 1, dims), :], p1, w, dims, False)
        load_in.wait()
        for first, count in blocks_of(own + 2, 2):
            block = conv_block(p1, kin, first, count, C, cell)
            for w in range(first, first + count):
                h = block[column(w - first, dims), :]
                hd_out[column(w + 1, dims), :] = h
                a = jnp.where(within(w, 1, k, dims), h * sigmoid(h), 0.0)
                store_hidden(a_out, w, a, dims)
                patches(a, p2, w, dims, False)
        load_out.wait()
        for first, count in blocks_after(own, blocks_of(own + 2, 2)):
            y_ref[first * cell : (first + count) * cell, :] = conv_block(
                p2, kout, first, count, D, cell
            )
        x1_out[...] = (slab[3 * cell : (3 + own) * cell, :] + y_ref[...]).astype(BF)
        e_rows = lo_out.shape[0]
        lo_out[...] = x1_out[:e_rows, :]
        hi_out[...] = x1_out[own * cell - e_rows :, :]

    @pl.when(role != 0)
    def _():
        for w in range(cols):
            patches(slab[column(w, dims), :], p1, w, dims, True)
        load_in.wait()
        load_out.wait()
        conv_back(p1, kout, own + 4, D, cell, hd_out)


def second_kernel(dims, n_edge, *refs):
    edges = 2 * n_edge + 1
    x_hbm = refs[:edges]
    hd_hbm, z_hbm, a_hbm, kin = refs[edges : edges + 4]
    g0_out, x_out, a_out, e_out = refs[edges + 4 : edges + 8]
    x1, hd, z, p1, p2, y_ref, sems = refs[edges + 8 :]
    cell, own, C, D = dims.cell, dims.own, dims.C, dims.D
    role, k = dims.my_role(), dims.my_slab()

    @pl.when(role == 0)
    def _():
        for copy in load([(z_hbm, x_out), (a_hbm, a_out)], sems):
            copy.wait()

    @pl.when(role != 0)
    def _():
        pairs, at = [], 0
        for ref in x_hbm:
            rows = ref.shape[0]
            pairs.append((ref, x1.at[pl.ds(at, rows), :]))
            at += rows
        copies = load(pairs + [(hd_hbm, hd), (z_hbm, z)], sems)
        for copy in copies[:edges]:
            copy.wait()
        x_out[...] = x1[2 * cell : (4 + own) * cell, :]
        for w in range(own + 6):
            patches(x1[column(w, dims), :].astype(F32), p1, w, dims, False)
        for copy in copies[edges:]:
            copy.wait()
        for first, count in blocks_of(own + 4, 2):
            block = conv_block(p1, kin, first, count, C, cell)
            for w in range(first, first + count):
                h = block[column(w - first, dims), :]
                ok = within(w, 2, k, dims)
                s = sigmoid(h)
                if 1 <= w < 3 + own:
                    store_hidden(a_out, w - 1, jnp.where(ok, h * s, 0.0), dims)
                e = hd[column(w, dims), :] * s * (1.0 + h * (1.0 - s))
                e = jnp.where(ok, e, 0.0)
                if 2 <= w < 2 + own:
                    e_out[column(w - 2, dims), :] = e.astype(BF)
                patches(e, p2, w, dims, True)
        for first, count in blocks_after(own + 2, blocks_of(own + 4, 2)):
            y_ref[first * cell : (first + count) * cell, :] = conv_back_block(
                p2, kin, first, count, C, cell
            )
        for w in range(own + 2):
            v = z[column(w, dims), :].astype(F32) + y_ref[column(w, dims), :]
            g0_out[column(w, dims), :] = jnp.where(within(w, 1, k, dims), v, 0.0).astype(BF)


def third_kernel(
    dims, g0_hbm, hd_hbm, x1_hbm, z_hbm, x_hbm, a_hbm, e_hbm, kout, e_out, g_out, sec_out,
    g0, hd, x1, z, x, a, p1, p2, y_ref, buf, sems,
):
    cell, own, C, D = dims.cell, dims.own, dims.C, dims.D
    role = dims.my_role()
    cols = own + 2
    mine = slice(cell, (1 + own) * cell)

    @pl.when(role == 0)
    def _():
        load_g, load_h, load_x = load(
            [(g0_hbm, g0), (hd_hbm, hd), (x1_hbm, x1)], sems
        )
        load_g.wait()
        g_out[...] = g0[mine, :]
        for w in range(cols):
            patches(g0[column(w, dims), :].astype(F32), p1, w, dims, True)
        load_h.wait()
        for first, count in blocks_of(own, 2):
            block = conv_back_block(p1, kout, first, count, D, cell)
            for w in range(first, first + count):
                e_out[column(w, dims), :] = gate(
                    block[column(w - first, dims), :], hd[column(w + 2, dims), :]
                ).astype(BF)
        load_x.wait()
        y_ref[...] = x1[...].astype(F32)

    @pl.when(role != 0)
    def _():
        load_a, load_x, load_g, load_e = load(
            [(a_hbm, a), (x_hbm, x), (z_hbm, z), (e_hbm, e_out)], sems
        )
        load_a.wait()
        for w in range(cols):
            patches(hidden_column(a, w, dims), p2, w, dims, False)
        conv(p2, kout, own, D, cell, y_ref)
        load_x.wait()
        y_ref[...] = y_ref[...] + x[mine, :].astype(F32)
        load_g.wait()
        g_out[...] = z[mine, :]
        load_e.wait()

    for d in range(dims.n):
        i, j = d // dims.rows, d % dims.rows
        for q in range(dims.fr):
            f, r = i * dims.f_here + q // dims.r_here, j * dims.r_here + q % dims.r_here
            at = (d * dims.fr + q) * own
            buf[at : at + own, :] = y_ref[pl.ds(f * dims.H + r, own, stride=cell), :]
    sec_out[...] = buf[...].astype(BF)


def unpack_kernel(dims, recv, out_ref, rbuf, buf):
    own = dims.own
    rbuf[...] = recv[...].astype(F32)
    for d in range(dims.n):
        at = dims.slab_of(d) * own
        for q in range(dims.fr):
            src = (d * dims.fr + q) * own
            buf[q, at : at + own, :] = rbuf[src : src + own, :]
    out_ref[...] = buf[...].astype(BF)


def chunk_of(dims, c):
    rows = 27 * c // dims.n
    return rows, -(-rows // 16) * 16


def grads_kernel(
    dims, in_masks, out_masks,
    x_mine, x_beside, a_mine, a_beside, e_mine, e_beside, g_mine, g_beside, keep, send,
    x, a, e, g, p_in, p_out, ut_in, ut_out, win_in, win_out, sems,
):
    cell, own, C, D = dims.cell, dims.own, dims.C, dims.D
    cols = own + 2
    copies = load(
        [
            (a_mine, a.at[0]), (a_beside, a.at[1]), (g_mine, g.at[0]), (g_beside, g.at[1]),
            (x_mine, x.at[0]), (x_beside, x.at[1]), (e_mine, e.at[0]), (e_beside, e.at[1]),
        ],
        sems,
    )

    def sums(c, p, column_of, u, ut, waits, win):
        for s in range(2):
            waits[s].wait()
            for w in range(cols):
                patches(column_of(s, w), p, s * cols + w, dims, False)
        for s in range(2):
            waits[2 + s].wait()
            ut[:, s * own * cell : (s + 1) * own * cell] = u[s].T
        for j in range(3):
            cells = [p[(s * cols + j) * cell : (s * cols + j + own) * cell, :] for s in range(2)]
            part = jnp.dot(ut[...], jnp.concatenate(cells, axis=0), preferred_element_type=F32)
            for ti in range(9):
                at = 3 * ti + j
                win[at * c : (at + 1) * c, :] = part[:, ti * c : (ti + 1) * c].T

    sums(D, p_out, lambda s, w: hidden_column(a.at[s], w, dims), g, ut_out, copies[:4], win_out)
    sums(
        C, p_in, lambda s, w: x[s, column(w, dims), :].astype(F32), e, ut_in, copies[4:], win_in
    )
    me = dims.my_device()

    def rows_of(win, mask, length):
        start = lax.bitwise_xor(me, mask) * length
        if length % 8 == 0:
            return win[pl.ds(pl.multiple_of(start, 8), length), :]
        size = -(-(length + 7) // 8) * 8
        base = lax.div(start, 8) * 8
        rows = win[pl.ds(pl.multiple_of(base, 8), size), :]
        return pltpu.roll(rows, size - (start - base), 0)[:length]

    length_in, padded_in = chunk_of(dims, C)
    length_out, padded_out = chunk_of(dims, D)
    for at, (in_mask, out_mask) in enumerate(zip(in_masks, out_masks)):
        pieces = [(0, rows_of(win_out, out_mask, length_out))]
        rows = rows_of(win_in, in_mask, length_in)
        for h in range(D // LANES):
            pieces.append((padded_out + h * padded_in, rows[:, h * LANES : (h + 1) * LANES]))
        for first, piece in pieces:
            if at % 2 == 0:
                keep[at // 2, first : first + piece.shape[0], :] = piece
            else:
                send[at // 2, first : first + piece.shape[0], :] = piece.astype(BF)


def split_kernel(padded_out, keep, got, out_keep, out_send, in_keep, in_send):
    for at in range(keep.shape[0]):
        v = keep[at] + got[at].astype(F32)
        for dst, sent, part in (
            (out_keep, out_send, v[:padded_out]), (in_keep, in_send, v[padded_out:])
        ):
            if at % 2 == 0:
                dst[at // 2] = part
            else:
                sent[at // 2] = part.astype(BF)


def final_kernel(dims, in_keep, in_got, out_keep, out_got, in_out, out_out):
    length, padded = chunk_of(dims, dims.C)
    halves = dims.D // LANES
    for h in range(halves):
        rows = slice(h * padded, h * padded + length)
        in_out[pl.ds(h, length, stride=halves), :] = in_keep[rows, :] + in_got[rows, :].astype(F32)
    length = out_out.shape[0]
    out_out[...] = out_keep[:length, :] + out_got[:length, :].astype(F32)


def call(dims, kernel, shapes, ins, scratch, cost, name, vmem=None):
    return pl.pallas_call(
        kernel,
        out_shape=shapes,
        in_specs=ins,
        out_specs=jax.tree.map(lambda _: pl.BlockSpec(memory_space=pltpu.VMEM), shapes),
        scratch_shapes=scratch,
        compiler_params=pltpu.CompilerParams(vmem_limit_bytes=vmem or dims.vmem),
        cost_estimate=pl.CostEstimate(flops=cost, bytes_accessed=4 << 20, transcendentals=0),
        name=name,
    )


def halving_steps(dims, order):
    steps = [("rows", 1)] + list(order)
    for axis, size in (("tm", dims.tm), ("rows", dims.rows)):
        apart = 4
        while apart < size:
            steps.append((axis, apart))
            apart *= 2
    steps = [(axis, apart, apart * (dims.rows if axis == "tm" else 1)) for axis, apart in steps]
    masks = [sum(s[2] for b, s in enumerate(steps) if m >> b & 1) for m in range(1 << len(steps))]
    return steps, masks


def group_swap(block, axis, apart):
    count = lax.axis_size(axis)
    return lax.ppermute(block, axis, [(i, i ^ apart) for i in range(count)])


def exchanged(blocks, n):
    got = lax.all_to_all(blocks.reshape(n, -1, blocks.shape[1]), ("tm", "rows"), 0, 0)
    return got.reshape(blocks.shape)


def edge_swap(dims, block, distance):
    pairs = []
    for k in range(dims.n):
        if 0 <= k + distance < dims.n:
            a, b = dims.slab_of(k), dims.n + dims.slab_of(k + distance)
            pairs += [(a, b), (b, a)]
    return lax.ppermute(block, ("segment", "tm", "rows"), pairs)


def added(keep, send, step):
    keep = keep + group_swap(send, step[0], step[1]).astype(F32)
    return keep[0::2], keep[1::2].astype(BF)


def on_device(shape, input_clip, cotangent, kernel_in, kernel_out):
    f_here, r_here, W, C = input_clip.shape
    D = kernel_in.shape[2]
    dims = Dims(shape, f_here, r_here, W, C, D)
    own, cell, n, fr = dims.own, dims.cell, dims.n, dims.fr
    kin, kout = kernel_in[0], kernel_out[0]
    kin_hbm, kout_hbm = (pltpu.with_memory_space_constraint(k, pltpu.HBM) for k in (kin, kout))
    vm = pl.BlockSpec(memory_space=pltpu.VMEM)
    hbm = pl.BlockSpec(memory_space=pltpu.HBM)
    sds = jax.ShapeDtypeStruct
    scr = pltpu.VMEM
    cols = own + 6
    conv_flops = 2 * 27 * C * D * cell
    e_cols, e_far = dims.edge(3)
    x_shape = sds(((own + 2) * cell, C), BF)
    a_shape = sds(((own + 2) * cell * (D // LANES), LANES), BF)

    send = call(
        dims, partial(pack_kernel, dims), sds((n * fr * cols, C), BF), [vm],
        [scr((fr, W + 16, C), F32), scr((n * fr * cols, C), F32)], 0, "pack",
    )(jnp.where(dims.my_role() == 0, input_clip, cotangent).reshape(fr, W, C))
    recv = exchanged(send, n)

    z, a1, x1, x1_lo, x1_hi, hd = call(
        dims, partial(first_kernel, dims),
        (
            x_shape, a_shape, sds((own * cell, C), BF), sds((e_cols * cell, C), BF),
            sds((e_cols * cell, C), BF), sds(((own + 4) * cell, D), F32),
        ),
        [hbm] * 3,
        [
            scr((n * fr * cols, C), BF), scr(kin.shape, BF), scr(kout.shape, BF),
            scr((n * fr * cols, C), F32), scr((cols * cell, C), F32),
            scr((cols * cell, 9 * C), BF), scr(((own + 2) * cell, 9 * D), BF),
            scr((own * cell, C), F32), pltpu.SemaphoreType.DMA((3,)),
        ],
        conv_flops * 2 * (own + 2), "first",
    )(recv, kin_hbm, kout_hbm)

    x1_there = group_swap(x1, "segment", 1)
    lefts = [edge_swap(dims, x1_hi, far) for far in range(e_far, 0, -1)]
    rights = [edge_swap(dims, x1_lo, -far) for far in range(1, e_far + 1)]

    g0, x2, a2, e1 = call(
        dims, partial(second_kernel, dims, e_far),
        (x_shape, x_shape, a_shape, sds((own * cell, D), BF)),
        [hbm] * (4 + 2 * e_far) + [vm],
        [
            scr((cols * cell, C), BF),
            scr(((own + 4) * cell, D), F32), scr(x_shape.shape, BF),
            scr((cols * cell, 9 * C), BF), scr(((own + 4) * cell, 9 * D), BF),
            scr(((own + 2) * cell, C), F32),
            pltpu.SemaphoreType.DMA((4 + 2 * e_far,)),
        ],
        conv_flops * 2 * (own + 2), "second",
    )(*lefts, x1_there, *rights, hd, z, a1, kin)

    g0_there = group_swap(g0, "segment", 1)
    a_beside = group_swap(a2, *OUT_GATHER)
    x_beside = group_swap(x2, *IN_GATHER)

    e, g, sec = call(
        dims, partial(third_kernel, dims),
        (sds((own * cell, D), BF), sds((own * cell, C), BF), sds((n * fr * own, C), BF)),
        [hbm] * 7 + [vm],
        [
            scr(g0.shape, BF), scr(hd.shape, F32), scr(x1.shape, BF),
            scr(x_shape.shape, BF), scr(x_shape.shape, BF), scr(a_shape.shape, BF),
            scr(((own + 2) * cell, 9 * C), BF), scr(((own + 2) * cell, 9 * D), BF),
            scr((own * cell, C), F32),
            scr((n * fr * own, C), F32), pltpu.SemaphoreType.DMA((5,)),
        ],
        conv_flops * own, "third",
    )(g0_there, hd, x1, z, x2, a2, e1, kout)
    e_beside = group_swap(e, *IN_GATHER)
    g_beside = group_swap(g, *OUT_GATHER)
    sec, x_beside = lax.optimization_barrier((sec, x_beside))
    back = exchanged(sec, n)
    e_beside, g_beside, back = lax.optimization_barrier((e_beside, g_beside, back))

    in_steps, in_masks = halving_steps(dims, IN_ORDER)
    out_steps, out_masks = halving_steps(dims, OUT_ORDER)
    half = len(in_masks) // 2
    padded_in, padded_out = chunk_of(dims, C)[1], chunk_of(dims, D)[1]
    both = padded_out + padded_in * (D // LANES)
    cells2 = 2 * (own + 2) * cell
    keep, sent = call(
        dims, partial(grads_kernel, dims, in_masks, out_masks),
        (sds((half, both, LANES), F32), sds((half, both, LANES), BF)),
        [hbm] * 8,
        [
            scr((2,) + x_shape.shape, BF), scr((2,) + a_shape.shape, BF),
            scr((2, own * cell, D), BF), scr((2, own * cell, C), BF),
            scr((cells2, 9 * C), BF), scr((cells2, 9 * D), BF),
            scr((D, 2 * own * cell), BF), scr((C, 2 * own * cell), BF),
            scr((27 * C + 64, D), F32), scr((27 * D + 64, C), F32),
            pltpu.SemaphoreType.DMA((8,)),
        ],
        2 * conv_flops * own, "grads", max(dims.vmem, 32 << 20),
    )(x2, x_beside, a2, a_beside, e, e_beside, g, g_beside)
    got = group_swap(sent, "rows", 1)
    quarter = half // 2
    out_keep, out_send, in_keep, in_send = call(
        dims, partial(split_kernel, padded_out),
        (
            sds((quarter, padded_out, LANES), F32), sds((quarter, padded_out, LANES), BF),
            sds((quarter, both - padded_out, LANES), F32),
            sds((quarter, both - padded_out, LANES), BF),
        ),
        [vm, vm], [], 0, "split",
    )(keep, got)
    for out_step, in_step in zip(out_steps[1:-1], in_steps[1:-1]):
        out_keep, out_send = added(out_keep, out_send, out_step)
        in_keep, in_send = added(in_keep, in_send, in_step)
    out_got = group_swap(out_send[0], *out_steps[-1][:2])
    in_got = group_swap(in_send[0], *in_steps[-1][:2])
    shard = 27 * C * D // n // LANES
    in_sum, out_sum = call(
        dims, partial(final_kernel, dims), (sds((shard, LANES), F32),) * 2, [vm] * 4, [], 0, "final",
    )(in_keep[0], in_got, out_keep[0], out_got)

    sections = call(
        dims, partial(unpack_kernel, dims), sds((fr, W, C), BF), [vm],
        [scr((n * fr * own, C), F32), scr((fr, W, C), F32)], 0, "unpack",
    )(back).reshape(f_here, r_here, W, C)
    return sections[None], in_sum.reshape(1, -1), out_sum.reshape(1, -1)


def solution(mesh):
    in_specs = (
        P("tm", "rows", None, None),
        P("tm", "rows", None, None),
        P("segment", None, None),
        P("segment", None, None),
    )
    out_specs = (
        P("segment", "tm", "rows", None, None),
        P("segment", ("tm", "rows")),
        P("segment", ("tm", "rows")),
    )
    return jax.shard_map(
        partial(on_device, dict(mesh.shape)), mesh=mesh, in_specs=in_specs,
        out_specs=out_specs, check_vma=False,
    )
```

```python
from functools import partial

import jax
import jax.numpy as jnp
from jax import lax
from jax.experimental import pallas as pl
from jax.experimental.pallas import tpu as pltpu
from jax.sharding import PartitionSpec as P

BF = jnp.bfloat16
F32 = jnp.float32
NT = (((1,), (1,)), ((), ()))
LANES = 128
IN_ORDER = (("tm", 1), ("rows", 2), ("tm", 2))
OUT_ORDER = (("rows", 2), ("tm", 1), ("tm", 2))


class Dims:
    def __init__(self, mesh, frames_here, rows_here, width, channels, hidden):
        self.tm, self.rows = mesh["tm"], mesh["rows"]
        self.n = self.tm * self.rows
        self.f_here, self.r_here = frames_here, rows_here
        self.fr = frames_here * rows_here
        self.F, self.H = self.tm * frames_here, self.rows * rows_here
        self.W, self.C, self.D = width, channels, hidden
        self.cell = self.F * self.H
        self.own = width // self.n
        self.vmem = (24 << 20) if self.cell <= 64 else (56 << 20)

    def slab_of(self, device):
        i, j = device // self.rows, device % self.rows
        return i * self.rows + (j if i % 2 == 0 else self.rows - 1 - j)

    def my_role(self):
        return lax.axis_index("segment")

    def my_device(self):
        return lax.axis_index("tm") * self.rows + lax.axis_index("rows")

    def my_slab(self):
        i, j = lax.axis_index("tm"), lax.axis_index("rows")
        return i * self.rows + jnp.where(lax.rem(i, 2) == 0, j, self.rows - 1 - j)

    def edge(self, halo):
        columns = min(self.own, halo)
        return columns, halo // columns


def sides_of(v, dims):
    v = v.reshape(dims.F, dims.H, v.shape[1])
    row = lax.broadcasted_iota(jnp.int32, v.shape, 1)
    before = jnp.where(row == 0, 0.0, pltpu.roll(v, 1, 1))
    after = jnp.where(row == dims.H - 1, 0.0, pltpu.roll(v, dims.H - 1, 1))
    return before, v, after


def patches(v, dst, at, dims, reverse):
    F, H, c = dims.F, dims.H, v.shape[1]
    sides = sides_of(v, dims)
    cell = dims.cell
    for i in range(3):
        s = sides[2 - i] if reverse else sides[i]
        whole = s.reshape(cell, c).astype(BF)
        for t in range(3):
            m = (2 - t) * H
            if m == 0:
                moved = whole
            elif m % 16 == 0:
                gap = jnp.zeros((m, c), BF)
                parts = [whole[m:], gap] if reverse else [gap, whole[: cell - m]]
                moved = jnp.concatenate(parts, axis=0)
            else:
                gap, flat = jnp.zeros((m, c), F32), s.reshape(cell, c)
                parts = [flat[m:], gap] if reverse else [gap, flat[: cell - m]]
                moved = jnp.concatenate(parts, axis=0).astype(BF)
            lane = (3 * t + i) * c
            dst[at * cell : (at + 1) * cell, lane : lane + c] = moved


def taps_of(k_ref, j, rows, axis):
    return jnp.concatenate(
        [k_ref[(3 * ti + j) * rows : (3 * ti + j + 1) * rows, :] for ti in range(9)], axis=axis
    )


def conv(p_ref, k_ref, columns, c, cell, acc_ref):
    for j in range(3):
        part = jnp.dot(
            p_ref[j * cell : (j + columns) * cell, :],
            taps_of(k_ref, j, c, 0),
            preferred_element_type=F32,
        )
        if j == 0:
            acc_ref[...] = part
        else:
            acc_ref[...] += part


def conv_block(p_ref, k_ref, first, columns, c, cell):
    total = None
    for j in range(3):
        part = jnp.dot(
            p_ref[(first + j) * cell : (first + j + columns) * cell, :],
            taps_of(k_ref, j, c, 0),
            preferred_element_type=F32,
        )
        total = part if total is None else total + part
    return total


def blocks_of(columns, count):
    size = -(-columns // count)
    return [(at, min(size, columns - at)) for at in range(0, columns, size)]


def blocks_after(columns, earlier):
    head = earlier[0][1] - 2
    if len(earlier) < 2 or head < 1 or head >= columns:
        return [(0, columns)]
    return [(0, head), (head, columns - head)]


def conv_back_block(p_ref, k_ref, first, columns, c_out, cell):
    total = None
    for j in range(3):
        part = lax.dot_general(
            p_ref[(first + 2 - j) * cell : (first + 2 - j + columns) * cell, :],
            taps_of(k_ref, j, c_out, 1),
            NT,
            preferred_element_type=F32,
        )
        total = part if total is None else total + part
    return total


def conv_back(p_ref, k_ref, columns, c_out, cell, acc_ref):
    for j in range(3):
        part = lax.dot_general(
            p_ref[(2 - j) * cell : (2 - j + columns) * cell, :],
            taps_of(k_ref, j, c_out, 1),
            NT,
            preferred_element_type=F32,
        )
        if j == 0:
            acc_ref[...] = part
        else:
            acc_ref[...] += part


def sigmoid(h):
    return 1.0 / (1.0 + jnp.exp(-h))


def gate(d, h):
    s = sigmoid(h)
    return d * s * (1.0 + h * (1.0 - s))


def column(w, dims):
    return slice(w * dims.cell, (w + 1) * dims.cell)


def within(w, halo, slab, dims):
    at = slab * dims.own + (w - halo)
    return jnp.logical_and(at >= 0, at < dims.W)


def load(pairs, sems):
    copies = [pltpu.make_async_copy(src, dst, sems.at[at]) for at, (src, dst) in enumerate(pairs)]
    for copy in copies:
        copy.start()
    return copies


def store_hidden(dst, w, a, dims):
    a = a.astype(BF)
    for h in range(dims.D // LANES):
        dst[column(h * (dims.own + 2) + w, dims), :] = a[:, h * LANES : (h + 1) * LANES]


def hidden_column(src, w, dims):
    parts = [src[column(h * (dims.own + 2) + w, dims), :] for h in range(dims.D // LANES)]
    return jnp.concatenate([part.astype(F32) for part in parts], axis=1)


def pack_kernel(dims, z_ref, out_ref, pad, buf):
    cols = dims.own + 6
    pad[:, :8, :] = jnp.zeros((dims.fr, 8, dims.C), F32)
    pad[:, 8 + dims.W :, :] = jnp.zeros((dims.fr, 8, dims.C), F32)
    pad[:, 8 : 8 + dims.W, :] = z_ref[...].astype(F32)
    for d in range(dims.n):
        start = dims.slab_of(d) * dims.own + 5
        for q in range(dims.fr):
            at = (d * dims.fr + q) * cols
            buf[at : at + cols, :] = pad[q, start : start + cols, :]
    out_ref[...] = buf[...].astype(BF)


def first_kernel(
    dims, recv, kin_hbm, kout_hbm, z_out, a_out, x1_out, lo_out, hi_out, hd_out,
    kin, kout, rbuf, slab, p1, p2, y_ref, sems,
):
    cell, own, C, D = dims.cell, dims.own, dims.C, dims.D
    load_in, load_out = load([(kin_hbm, kin), (kout_hbm, kout)], sems)
    cols = own + 6
    role, k = dims.my_role(), dims.my_slab()
    rbuf[...] = recv[...].astype(F32)
    for s in range(dims.n):
        i, j = s // dims.rows, s % dims.rows
        for q in range(dims.fr):
            f, r = i * dims.f_here + q // dims.r_here, j * dims.r_here + q % dims.r_here
            at = (s * dims.fr + q) * cols
            slab[pl.ds(f * dims.H + r, cols, stride=cell), :] = rbuf[at : at + cols, :]
    z_out[...] = slab[2 * cell : (4 + own) * cell, :].astype(BF)

    @pl.when(role == 0)
    def _():
        for w in range(own + 4):
            patches(slab[column(w + 1, dims), :], p1, w, dims, False)
        load_in.wait()
        for first, count in blocks_of(own + 2, 2):
            block = conv_block(p1, kin, first, count, C, cell)
            for w in range(first, first + count):
                h = block[column(w - first, dims), :]
                hd_out[column(w + 1, dims), :] = h
                a = jnp.where(within(w, 1, k, dims), h * sigmoid(h), 0.0)
                store_hidden(a_out, w, a, dims)
                patches(a, p2, w, dims, False)
        load_out.wait()
        for first, count in blocks_after(own, blocks_of(own + 2, 2)):
            y_ref[first * cell : (first + count) * cell, :] = conv_block(
                p2, kout, first, count, D, cell
            )
        x1_out[...] = (slab[3 * cell : (3 + own) * cell, :] + y_ref[...]).astype(BF)
        e_rows = lo_out.shape[0]
        lo_out[...] = x1_out[:e_rows, :]
        hi_out[...] = x1_out[own * cell - e_rows :, :]

    @pl.when(role != 0)
    def _():
        for w in range(cols):
            patches(slab[column(w, dims), :], p1, w, dims, True)
        load_in.wait()
        load_out.wait()
        conv_back(p1, kout, own + 4, D, cell, hd_out)


def second_kernel(dims, n_edge, *refs):
    edges = 2 * n_edge + 1
    pieces = refs[:edges]
    hd, z, _, kin = refs[edges : edges + 4]
    g0_out, x_out, a_out, e_out = refs[edges + 4 : edges + 8]
    p1, p2, y_ref, sems = refs[edges + 8 :]
    cell, own, C, D = dims.cell, dims.own, dims.C, dims.D
    role, k = dims.my_role(), dims.my_slab()

    @pl.when(role == 0)
    def _():
        for copy in load([(z, x_out), (refs[edges + 2], a_out)], sems):
            copy.wait()

    @pl.when(role != 0)
    def _():
        columns = [(ref, at) for ref in pieces for at in range(ref.shape[0] // cell)]
        for w, (ref, at) in enumerate(columns):
            v = ref[column(at, dims), :]
            if 2 <= w < own + 4:
                x_out[column(w - 2, dims), :] = v
            patches(v.astype(F32), p1, w, dims, False)
        for first, count in blocks_of(own + 4, 2):
            block = conv_block(p1, kin, first, count, C, cell)
            for w in range(first, first + count):
                h = block[column(w - first, dims), :]
                ok = within(w, 2, k, dims)
                s = sigmoid(h)
                if 1 <= w < 3 + own:
                    store_hidden(a_out, w - 1, jnp.where(ok, h * s, 0.0), dims)
                e = hd[column(w, dims), :] * s * (1.0 + h * (1.0 - s))
                e = jnp.where(ok, e, 0.0)
                if 2 <= w < 2 + own:
                    e_out[column(w - 2, dims), :] = e.astype(BF)
                patches(e, p2, w, dims, True)
        for first, count in blocks_after(own + 2, blocks_of(own + 4, 2)):
            y_ref[first * cell : (first + count) * cell, :] = conv_back_block(
                p2, kin, first, count, C, cell
            )
        for w in range(own + 2):
            v = z[column(w, dims), :].astype(F32) + y_ref[column(w, dims), :]
            g0_out[column(w, dims), :] = jnp.where(within(w, 1, k, dims), v, 0.0).astype(BF)


def third_kernel(
    dims, g0, hd, x1, z, x, a, e_in, kout, e_out, g_out, sec_out,
    p1, p2, y_ref, buf,
):
    cell, own, C, D = dims.cell, dims.own, dims.C, dims.D
    role = dims.my_role()
    cols = own + 2
    mine = slice(cell, (1 + own) * cell)

    @pl.when(role == 0)
    def _():
        g_out[...] = g0[mine, :]
        for w in range(cols):
            patches(g0[column(w, dims), :].astype(F32), p1, w, dims, True)
        for first, count in blocks_of(own, 2):
            block = conv_back_block(p1, kout, first, count, D, cell)
            for w in range(first, first + count):
                e_out[column(w, dims), :] = gate(
                    block[column(w - first, dims), :], hd[column(w + 2, dims), :]
                ).astype(BF)
        y_ref[...] = x1[...].astype(F32)

    @pl.when(role != 0)
    def _():
        for w in range(cols):
            patches(hidden_column(a, w, dims), p2, w, dims, False)
        conv(p2, kout, own, D, cell, y_ref)
        y_ref[...] = y_ref[...] + x[mine, :].astype(F32)
        g_out[...] = z[mine, :]
        e_out[...] = e_in[...]

    for d in range(dims.n):
        i, j = d // dims.rows, d % dims.rows
        for q in range(dims.fr):
            f, r = i * dims.f_here + q // dims.r_here, j * dims.r_here + q % dims.r_here
            at = (d * dims.fr + q) * own
            buf[at : at + own, :] = y_ref[pl.ds(f * dims.H + r, own, stride=cell), :]
    sec_out[...] = buf[...].astype(BF)


def unpack_kernel(dims, recv, out_ref, rbuf, buf):
    own = dims.own
    rbuf[...] = recv[...].astype(F32)
    for d in range(dims.n):
        at = dims.slab_of(d) * own
        for q in range(dims.fr):
            src = (d * dims.fr + q) * own
            buf[q, at : at + own, :] = rbuf[src : src + own, :]
    out_ref[...] = buf[...].astype(BF)


def chunk_of(dims, c):
    rows = 27 * c // dims.n
    return rows, -(-rows // 16) * 16


def grad_kernel(
    dims, c, masks, v_mine, v_beside, u_mine, u_beside, keep, send, p, ut, win
):
    cell, own = dims.cell, dims.own
    cols = own + 2
    for s, v in enumerate((v_mine, v_beside)):
        for w in range(cols):
            if c == dims.C:
                values = v[column(w, dims), :].astype(F32)
            else:
                values = hidden_column(v, w, dims)
            patches(values, p, s * cols + w, dims, False)
    for s, u in enumerate((u_mine, u_beside)):
        ut[:, s * own * cell : (s + 1) * own * cell] = u[...].T
    for j in range(3):
        cells = [p[(s * cols + j) * cell : (s * cols + j + own) * cell, :] for s in range(2)]
        part = jnp.dot(ut[...], jnp.concatenate(cells, axis=0), preferred_element_type=F32)
        for ti in range(9):
            at = 3 * ti + j
            win[at * c : (at + 1) * c, :] = part[:, ti * c : (ti + 1) * c].T
    me = dims.my_device()
    length, padded = chunk_of(dims, c)

    def rows_of(mask):
        start = lax.bitwise_xor(me, mask) * length
        if length % 8 == 0:
            return win[pl.ds(pl.multiple_of(start, 8), length), :]
        size = -(-(length + 7) // 8) * 8
        base = lax.div(start, 8) * 8
        rows = win[pl.ds(pl.multiple_of(base, 8), size), :]
        return pltpu.roll(rows, size - (start - base), 0)[:length]

    for at, mask in enumerate(masks):
        rows = rows_of(mask)
        for h in range(rows.shape[1] // LANES):
            piece = rows[:, h * LANES : (h + 1) * LANES]
            to = slice(h * padded, h * padded + length)
            if at % 2 == 0:
                keep[at // 2, to, :] = piece
            else:
                send[at // 2, to, :] = piece.astype(BF)


def add_kernel(keep, got, keep_out, send_out):
    for at in range(keep.shape[0]):
        v = keep[at] + got[at].astype(F32)
        if at % 2 == 0:
            keep_out[at // 2] = v
        else:
            send_out[at // 2] = v.astype(BF)


def final_kernel(dims, in_keep, in_got, out_keep, out_got, in_out, out_out):
    length, padded = chunk_of(dims, dims.C)
    halves = dims.D // LANES
    for h in range(halves):
        rows = slice(h * padded, h * padded + length)
        in_out[pl.ds(h, length, stride=halves), :] = in_keep[rows, :] + in_got[rows, :].astype(F32)
    length = out_out.shape[0]
    out_out[...] = out_keep[:length, :] + out_got[:length, :].astype(F32)


def call(dims, kernel, shapes, ins, scratch, cost, name, vmem=None):
    return pl.pallas_call(
        kernel,
        out_shape=shapes,
        in_specs=ins,
        out_specs=jax.tree.map(lambda _: pl.BlockSpec(memory_space=pltpu.VMEM), shapes),
        scratch_shapes=scratch,
        compiler_params=pltpu.CompilerParams(vmem_limit_bytes=vmem or dims.vmem),
        cost_estimate=pl.CostEstimate(flops=cost, bytes_accessed=4 << 20, transcendentals=0),
        name=name,
    )


def halving_steps(dims, order):
    steps = list(order)
    for axis, size in (("tm", dims.tm), ("rows", dims.rows)):
        apart = 4
        while apart < size:
            steps.append((axis, apart))
            apart *= 2
    steps = [(axis, apart, apart * (dims.rows if axis == "tm" else 1)) for axis, apart in steps]
    masks = [sum(s[2] for b, s in enumerate(steps) if m >> b & 1) for m in range(1 << len(steps))]
    return steps, masks


def group_swap(block, axis, apart):
    count = lax.axis_size(axis)
    return lax.ppermute(block, axis, [(i, i ^ apart) for i in range(count)])


def exchanged(blocks, n):
    got = lax.all_to_all(blocks.reshape(n, -1, blocks.shape[1]), ("tm", "rows"), 0, 0)
    return got.reshape(blocks.shape)


def edge_swap(dims, block, distance):
    pairs = []
    for k in range(dims.n):
        if 0 <= k + distance < dims.n:
            a, b = dims.slab_of(k), dims.n + dims.slab_of(k + distance)
            pairs += [(a, b), (b, a)]
    return lax.ppermute(block, ("segment", "tm", "rows"), pairs)


def added(dims, keep, send, step, name, also=None):
    got = group_swap(send, step[0], step[1])
    if also is not None:
        got, also = lax.optimization_barrier((got, also))
    half, rows, lanes = keep.shape
    vm = pl.BlockSpec(memory_space=pltpu.VMEM)
    shape = (half // 2, rows, lanes)
    keep, send = call(
        dims, add_kernel,
        (jax.ShapeDtypeStruct(shape, F32), jax.ShapeDtypeStruct(shape, BF)), [vm, vm], [], 0, name,
    )(keep, got)
    return keep, send, also


def on_device(shape, input_clip, cotangent, kernel_in, kernel_out):
    f_here, r_here, W, C = input_clip.shape
    D = kernel_in.shape[2]
    dims = Dims(shape, f_here, r_here, W, C, D)
    own, cell, n, fr = dims.own, dims.cell, dims.n, dims.fr
    kin, kout = kernel_in[0], kernel_out[0]
    kin_hbm, kout_hbm = (pltpu.with_memory_space_constraint(k, pltpu.HBM) for k in (kin, kout))
    vm = pl.BlockSpec(memory_space=pltpu.VMEM)
    hbm = pl.BlockSpec(memory_space=pltpu.HBM)
    sds = jax.ShapeDtypeStruct
    scr = pltpu.VMEM
    cols = own + 6
    conv_flops = 2 * 27 * C * D * cell
    e_cols, e_far = dims.edge(3)
    x_shape = sds(((own + 2) * cell, C), BF)
    a_shape = sds(((own + 2) * cell * (D // LANES), LANES), BF)

    send = call(
        dims, partial(pack_kernel, dims), sds((n * fr * cols, C), BF), [vm],
        [scr((fr, W + 16, C), F32), scr((n * fr * cols, C), F32)], 0, "pack",
    )(jnp.where(dims.my_role() == 0, input_clip, cotangent).reshape(fr, W, C))
    recv = exchanged(send, n)

    z, a1, x1, x1_lo, x1_hi, hd = call(
        dims, partial(first_kernel, dims),
        (
            x_shape, a_shape, sds((own * cell, C), BF), sds((e_cols * cell, C), BF),
            sds((e_cols * cell, C), BF), sds(((own + 4) * cell, D), F32),
        ),
        [vm, hbm, hbm],
        [
            scr(kin.shape, BF), scr(kout.shape, BF),
            scr((n * fr * cols, C), F32), scr((cols * cell, C), F32),
            scr((cols * cell, 9 * C), BF), scr(((own + 2) * cell, 9 * D), BF),
            scr((own * cell, C), F32), pltpu.SemaphoreType.DMA((2,)),
        ],
        conv_flops * 2 * (own + 2), "first",
    )(recv, kin_hbm, kout_hbm)

    x1_there = group_swap(x1, "segment", 1)
    lefts = [edge_swap(dims, x1_hi, far) for far in range(e_far, 0, -1)]
    rights = [edge_swap(dims, x1_lo, -far) for far in range(1, e_far + 1)]

    g0, x2, a2, e1 = call(
        dims, partial(second_kernel, dims, e_far),
        (x_shape, x_shape, a_shape, sds((own * cell, D), BF)),
        [vm] * (5 + 2 * e_far),
        [
            scr((cols * cell, 9 * C), BF), scr(((own + 4) * cell, 9 * D), BF),
            scr(((own + 2) * cell, C), F32),
            pltpu.SemaphoreType.DMA((2,)),
        ],
        conv_flops * 2 * (own + 2), "second",
    )(*lefts, x1_there, *rights, hd, z, a1, kin)

    g0_there = group_swap(g0, "segment", 1)
    a_beside = group_swap(a2, "rows", 1)
    x_beside = group_swap(x2, "rows", 1)

    e, g, sec = call(
        dims, partial(third_kernel, dims),
        (sds((own * cell, D), BF), sds((own * cell, C), BF), sds((n * fr * own, C), BF)),
        [vm] * 8,
        [
            scr(((own + 2) * cell, 9 * C), BF), scr(((own + 2) * cell, 9 * D), BF),
            scr((own * cell, C), F32),
            scr((n * fr * own, C), F32),
        ],
        conv_flops * own, "third",
    )(g0_there, hd, x1, z, x2, a2, e1, kout)
    e_beside = group_swap(e, "rows", 1)
    g_beside = group_swap(g, "rows", 1)

    in_steps, in_masks = halving_steps(dims, IN_ORDER)
    out_steps, out_masks = halving_steps(dims, OUT_ORDER)
    half = len(in_masks) // 2

    def grad(c, c_out, masks, v, v_beside, u, u_beside, name):
        rows = chunk_of(dims, c)[1] * (c_out // LANES)
        return call(
            dims, partial(grad_kernel, dims, c, masks),
            (sds((half, rows, LANES), F32), sds((half, rows, LANES), BF)),
            [vm] * 4,
            [
                scr((2 * (own + 2) * cell, 9 * c), BF), scr((c_out, 2 * own * cell), BF),
                scr((27 * c + 64, c_out), F32),
            ],
            conv_flops * own, name,
        )(v, v_beside, u, u_beside)

    out_keep, out_send = grad(D, C, out_masks, a2, a_beside, g, g_beside, "grad_out")
    e, e_beside, out_send = lax.optimization_barrier((e, e_beside, out_send))
    in_keep, in_send = grad(C, D, in_masks, x2, x_beside, e, e_beside, "grad_in")
    sec, in_keep, out_keep = lax.optimization_barrier((sec, in_keep, out_keep))
    back = exchanged(sec, n)
    for at in range(len(in_steps) - 1):
        out_keep, out_send, back_out = added(
            dims, out_keep, out_send, out_steps[at], "add_out", back if False else None
        )
        in_keep, in_send, back_in = added(
            dims, in_keep, in_send, in_steps[at], "add_in", back if at == 1 else None
        )
        back = back if back_in is None else back_in
    out_got = group_swap(out_send[0], *out_steps[-1][:2])
    in_got = group_swap(in_send[0], *in_steps[-1][:2])
    shard = 27 * C * D // n // LANES
    in_sum, out_sum = call(
        dims, partial(final_kernel, dims), (sds((shard, LANES), F32),) * 2, [vm] * 4, [], 0, "final",
    )(in_keep[0], in_got, out_keep[0], out_got)

    sections = call(
        dims, partial(unpack_kernel, dims), sds((fr, W, C), BF), [vm],
        [scr((n * fr * own, C), F32), scr((fr, W, C), F32)], 0, "unpack",
    )(back).reshape(f_here, r_here, W, C)
    return sections[None], in_sum.reshape(1, -1), out_sum.reshape(1, -1)


def solution(mesh):
    in_specs = (
        P("tm", "rows", None, None),
        P("tm", "rows", None, None),
        P("segment", None, None),
        P("segment", None, None),
    )
    out_specs = (
        P("segment", "tm", "rows", None, None),
        P("segment", ("tm", "rows")),
        P("segment", ("tm", "rows")),
    )
    return jax.shard_map(
        partial(on_device, dict(mesh.shape)), mesh=mesh, in_specs=in_specs,
        out_specs=out_specs, check_vma=False,
    )
```

```python
from functools import partial

import jax
import jax.numpy as jnp
from jax import lax
from jax.experimental import pallas as pl
from jax.experimental.pallas import tpu as pltpu
from jax.sharding import PartitionSpec as P

BF = jnp.bfloat16
F32 = jnp.float32
NT = (((1,), (1,)), ((), ()))
LANES = 128
IN_ORDER = (("tm", 1), ("rows", 2), ("tm", 2))
OUT_ORDER = (("rows", 2), ("tm", 1), ("tm", 2))


class Dims:
    def __init__(self, mesh, frames_here, rows_here, width, channels, hidden):
        self.tm, self.rows = mesh["tm"], mesh["rows"]
        self.n = self.tm * self.rows
        self.f_here, self.r_here = frames_here, rows_here
        self.fr = frames_here * rows_here
        self.F, self.H = self.tm * frames_here, self.rows * rows_here
        self.W, self.C, self.D = width, channels, hidden
        self.cell = self.F * self.H
        self.own = width // self.n
        self.vmem = (24 << 20) if self.cell <= 64 else (56 << 20)

    def slab_of(self, device):
        i, j = device // self.rows, device % self.rows
        return i * self.rows + (j if i % 2 == 0 else self.rows - 1 - j)

    def my_role(self):
        return lax.axis_index("segment")

    def my_device(self):
        return lax.axis_index("tm") * self.rows + lax.axis_index("rows")

    def my_slab(self):
        i, j = lax.axis_index("tm"), lax.axis_index("rows")
        return i * self.rows + jnp.where(lax.rem(i, 2) == 0, j, self.rows - 1 - j)

    def edge(self, halo):
        columns = min(self.own, halo)
        return columns, halo // columns


def sides_of(v, dims):
    v = v.reshape(dims.F, dims.H, v.shape[1])
    row = lax.broadcasted_iota(jnp.int32, v.shape, 1)
    before = jnp.where(row == 0, 0.0, pltpu.roll(v, 1, 1))
    after = jnp.where(row == dims.H - 1, 0.0, pltpu.roll(v, dims.H - 1, 1))
    return before, v, after


def patches(v, dst, at, dims, reverse):
    F, H, c = dims.F, dims.H, v.shape[1]
    sides = sides_of(v, dims)
    cell = dims.cell
    for i in range(3):
        s = sides[2 - i] if reverse else sides[i]
        whole = s.reshape(cell, c).astype(BF)
        for t in range(3):
            m = (2 - t) * H
            if m == 0:
                moved = whole
            elif m % 16 == 0:
                gap = jnp.zeros((m, c), BF)
                parts = [whole[m:], gap] if reverse else [gap, whole[: cell - m]]
                moved = jnp.concatenate(parts, axis=0)
            else:
                gap, flat = jnp.zeros((m, c), F32), s.reshape(cell, c)
                parts = [flat[m:], gap] if reverse else [gap, flat[: cell - m]]
                moved = jnp.concatenate(parts, axis=0).astype(BF)
            lane = (3 * t + i) * c
            dst[at * cell : (at + 1) * cell, lane : lane + c] = moved


def taps_of(k_ref, j, rows, axis):
    return jnp.concatenate(
        [k_ref[(3 * ti + j) * rows : (3 * ti + j + 1) * rows, :] for ti in range(9)], axis=axis
    )


def conv(p_ref, k_ref, columns, c, cell, acc_ref):
    for j in range(3):
        part = jnp.dot(
            p_ref[j * cell : (j + columns) * cell, :],
            taps_of(k_ref, j, c, 0),
            preferred_element_type=F32,
        )
        if j == 0:
            acc_ref[...] = part
        else:
            acc_ref[...] += part


def conv_block(p_ref, k_ref, first, columns, c, cell):
    total = None
    for j in range(3):
        part = jnp.dot(
            p_ref[(first + j) * cell : (first + j + columns) * cell, :],
            taps_of(k_ref, j, c, 0),
            preferred_element_type=F32,
        )
        total = part if total is None else total + part
    return total


def blocks_of(columns, count):
    size = -(-columns // count)
    return [(at, min(size, columns - at)) for at in range(0, columns, size)]


def blocks_after(columns, earlier):
    head = earlier[0][1] - 2
    if len(earlier) < 2 or head < 1 or head >= columns:
        return [(0, columns)]
    return [(0, head), (head, columns - head)]


def conv_back_block(p_ref, k_ref, first, columns, c_out, cell):
    total = None
    for j in range(3):
        part = lax.dot_general(
            p_ref[(first + 2 - j) * cell : (first + 2 - j + columns) * cell, :],
            taps_of(k_ref, j, c_out, 1),
            NT,
            preferred_element_type=F32,
        )
        total = part if total is None else total + part
    return total


def conv_back(p_ref, k_ref, columns, c_out, cell, acc_ref):
    for j in range(3):
        part = lax.dot_general(
            p_ref[(2 - j) * cell : (2 - j + columns) * cell, :],
            taps_of(k_ref, j, c_out, 1),
            NT,
            preferred_element_type=F32,
        )
        if j == 0:
            acc_ref[...] = part
        else:
            acc_ref[...] += part


def sigmoid(h):
    return 1.0 / (1.0 + jnp.exp(-h))


def gate(d, h):
    s = sigmoid(h)
    return d * s * (1.0 + h * (1.0 - s))


def column(w, dims):
    return slice(w * dims.cell, (w + 1) * dims.cell)


def within(w, halo, slab, dims):
    at = slab * dims.own + (w - halo)
    return jnp.logical_and(at >= 0, at < dims.W)


def load(pairs, sems):
    copies = [pltpu.make_async_copy(src, dst, sems.at[at]) for at, (src, dst) in enumerate(pairs)]
    for copy in copies:
        copy.start()
    return copies


def store_hidden(dst, w, a, dims):
    a = a.astype(BF)
    for h in range(dims.D // LANES):
        dst[column(h * (dims.own + 2) + w, dims), :] = a[:, h * LANES : (h + 1) * LANES]


def hidden_column(src, w, dims):
    parts = [src[column(h * (dims.own + 2) + w, dims), :] for h in range(dims.D // LANES)]
    return jnp.concatenate([part.astype(F32) for part in parts], axis=1)


def pack_kernel(dims, z_ref, out_ref, pad, buf):
    cols = dims.own + 6
    pad[:, :8, :] = jnp.zeros((dims.fr, 8, dims.C), F32)
    pad[:, 8 + dims.W :, :] = jnp.zeros((dims.fr, 8, dims.C), F32)
    pad[:, 8 : 8 + dims.W, :] = z_ref[...].astype(F32)
    for d in range(dims.n):
        start = dims.slab_of(d) * dims.own + 5
        for q in range(dims.fr):
            at = (d * dims.fr + q) * cols
            buf[at : at + cols, :] = pad[q, start : start + cols, :]
    out_ref[...] = buf[...].astype(BF)


def first_kernel(
    dims, recv, kin_hbm, kout_hbm, z_out, a_out, x1_out, lo_out, hi_out, hd_out,
    kin, kout, rbuf, slab, p1, p2, y_ref, sems,
):
    cell, own, C, D = dims.cell, dims.own, dims.C, dims.D
    load_in, load_out = load([(kin_hbm, kin), (kout_hbm, kout)], sems)
    cols = own + 6
    role, k = dims.my_role(), dims.my_slab()
    rbuf[...] = recv[...].astype(F32)
    for s in range(dims.n):
        i, j = s // dims.rows, s % dims.rows
        for q in range(dims.fr):
            f, r = i * dims.f_here + q // dims.r_here, j * dims.r_here + q % dims.r_here
            at = (s * dims.fr + q) * cols
            slab[pl.ds(f * dims.H + r, cols, stride=cell), :] = rbuf[at : at + cols, :]
    z_out[...] = slab[2 * cell : (4 + own) * cell, :].astype(BF)

    @pl.when(role == 0)
    def _():
        for w in range(own + 4):
            patches(slab[column(w + 1, dims), :], p1, w, dims, False)
        load_in.wait()
        for first, count in blocks_of(own + 2, 2):
            block = conv_block(p1, kin, first, count, C, cell)
            for w in range(first, first + count):
                h = block[column(w - first, dims), :]
                hd_out[column(w + 1, dims), :] = h
                a = jnp.where(within(w, 1, k, dims), h * sigmoid(h), 0.0)
                store_hidden(a_out, w, a, dims)
                patches(a, p2, w, dims, False)
        load_out.wait()
        for first, count in blocks_after(own, blocks_of(own + 2, 2)):
            y_ref[first * cell : (first + count) * cell, :] = conv_block(
                p2, kout, first, count, D, cell
            )
        x1_out[...] = (slab[3 * cell : (3 + own) * cell, :] + y_ref[...]).astype(BF)
        e_rows = lo_out.shape[0]
        lo_out[...] = x1_out[:e_rows, :]
        hi_out[...] = x1_out[own * cell - e_rows :, :]

    @pl.when(role != 0)
    def _():
        for w in range(cols):
            patches(slab[column(w, dims), :], p1, w, dims, True)
        load_in.wait()
        load_out.wait()
        conv_back(p1, kout, own + 4, D, cell, hd_out)


def second_kernel(dims, n_edge, *refs):
    edges = 2 * n_edge + 1
    pieces = refs[:edges]
    hd, z, _, kin = refs[edges : edges + 4]
    g0_out, x_out, a_out, e_out = refs[edges + 4 : edges + 8]
    p1, p2, y_ref, sems = refs[edges + 8 :]
    cell, own, C, D = dims.cell, dims.own, dims.C, dims.D
    role, k = dims.my_role(), dims.my_slab()

    @pl.when(role == 0)
    def _():
        for copy in load([(z, x_out), (refs[edges + 2], a_out)], sems):
            copy.wait()

    @pl.when(role != 0)
    def _():
        columns = [(ref, at) for ref in pieces for at in range(ref.shape[0] // cell)]
        for w, (ref, at) in enumerate(columns):
            v = ref[column(at, dims), :]
            if 2 <= w < own + 4:
                x_out[column(w - 2, dims), :] = v
            patches(v.astype(F32), p1, w, dims, False)
        for first, count in blocks_of(own + 4, 2):
            block = conv_block(p1, kin, first, count, C, cell)
            for w in range(first, first + count):
                h = block[column(w - first, dims), :]
                ok = within(w, 2, k, dims)
                s = sigmoid(h)
                if 1 <= w < 3 + own:
                    store_hidden(a_out, w - 1, jnp.where(ok, h * s, 0.0), dims)
                e = hd[column(w, dims), :] * s * (1.0 + h * (1.0 - s))
                e = jnp.where(ok, e, 0.0)
                if 2 <= w < 2 + own:
                    e_out[column(w - 2, dims), :] = e.astype(BF)
                patches(e, p2, w, dims, True)
        for first, count in blocks_after(own + 2, blocks_of(own + 4, 2)):
            y_ref[first * cell : (first + count) * cell, :] = conv_back_block(
                p2, kin, first, count, C, cell
            )
        for w in range(own + 2):
            v = z[column(w, dims), :].astype(F32) + y_ref[column(w, dims), :]
            g0_out[column(w, dims), :] = jnp.where(within(w, 1, k, dims), v, 0.0).astype(BF)


def third_kernel(
    dims, g0, hd, x1, z, x, a, e_in, kout, e_out, g_out, sec_out,
    p1, p2, y_ref, buf,
):
    cell, own, C, D = dims.cell, dims.own, dims.C, dims.D
    role = dims.my_role()
    cols = own + 2
    mine = slice(cell, (1 + own) * cell)

    @pl.when(role == 0)
    def _():
        g_out[...] = g0[mine, :]
        for w in range(cols):
            patches(g0[column(w, dims), :].astype(F32), p1, w, dims, True)
        for first, count in blocks_of(own, 2):
            block = conv_back_block(p1, kout, first, count, D, cell)
            for w in range(first, first + count):
                e_out[column(w, dims), :] = gate(
                    block[column(w - first, dims), :], hd[column(w + 2, dims), :]
                ).astype(BF)
        y_ref[...] = x1[...].astype(F32)

    @pl.when(role != 0)
    def _():
        for w in range(cols):
            patches(hidden_column(a, w, dims), p2, w, dims, False)
        conv(p2, kout, own, D, cell, y_ref)
        y_ref[...] = y_ref[...] + x[mine, :].astype(F32)
        g_out[...] = z[mine, :]
        e_out[...] = e_in[...]

    for d in range(dims.n):
        i, j = d // dims.rows, d % dims.rows
        for q in range(dims.fr):
            f, r = i * dims.f_here + q // dims.r_here, j * dims.r_here + q % dims.r_here
            at = (d * dims.fr + q) * own
            buf[at : at + own, :] = y_ref[pl.ds(f * dims.H + r, own, stride=cell), :]
    sec_out[...] = buf[...].astype(BF)


def unpack_kernel(dims, recv, out_ref, rbuf, buf):
    own = dims.own
    rbuf[...] = recv[...].astype(F32)
    for d in range(dims.n):
        at = dims.slab_of(d) * own
        for q in range(dims.fr):
            src = (d * dims.fr + q) * own
            buf[q, at : at + own, :] = rbuf[src : src + own, :]
    out_ref[...] = buf[...].astype(BF)


def chunk_of(dims, c):
    rows = 27 * c // dims.n
    return rows, -(-rows // 16) * 16


def streams_of(dims, c, c_out):
    padded = chunk_of(dims, c)[1]
    if c_out > LANES:
        return [(padded, 0)] * (c_out // LANES)
    head = -(-padded // 32) * 16
    return [(head, 0), (padded - head, head)] if padded > head else [(padded, 0)]


def grad_kernel(dims, c, masks, v_mine, v_beside, u_mine, u_beside, *refs):
    cell, own = dims.cell, dims.own
    cols = own + 2
    p, ut, win = refs[-3:]
    streams = streams_of(dims, c, ut.shape[0])
    for s, v in enumerate((v_mine, v_beside)):
        for w in range(cols):
            if c == dims.C:
                values = v[column(w, dims), :].astype(F32)
            else:
                values = hidden_column(v, w, dims)
            patches(values, p, s * cols + w, dims, False)
    for s, u in enumerate((u_mine, u_beside)):
        ut[:, s * own * cell : (s + 1) * own * cell] = u[...].T
    for j in range(3):
        cells = [p[(s * cols + j) * cell : (s * cols + j + own) * cell, :] for s in range(2)]
        part = jnp.dot(ut[...], jnp.concatenate(cells, axis=0), preferred_element_type=F32)
        for ti in range(9):
            at = 3 * ti + j
            win[at * c : (at + 1) * c, :] = part[:, ti * c : (ti + 1) * c].T
    me = dims.my_device()
    length, _ = chunk_of(dims, c)

    def rows_of(mask):
        start = lax.bitwise_xor(me, mask) * length
        if length % 8 == 0:
            return win[pl.ds(pl.multiple_of(start, 8), length), :]
        size = -(-(length + 7) // 8) * 8
        base = lax.div(start, 8) * 8
        rows = win[pl.ds(pl.multiple_of(base, 8), size), :]
        return pltpu.roll(rows, size - (start - base), 0)[:length]

    for at, mask in enumerate(masks):
        rows = rows_of(mask)
        for b, (count, head) in enumerate(streams):
            lane = b * LANES if rows.shape[1] > LANES else 0
            piece = rows[head : min(head + count, length), lane : lane + LANES]
            to = slice(0, piece.shape[0])
            if at % 2 == 0:
                refs[2 * b][at // 2, to, :] = piece
            else:
                refs[2 * b + 1][at // 2, to, :] = piece.astype(BF)


def add_kernel(keep, got, keep_out, send_out):
    for at in range(keep.shape[0]):
        v = keep[at] + got[at].astype(F32)
        if at % 2 == 0:
            keep_out[at // 2] = v
        else:
            send_out[at // 2] = v.astype(BF)


def final_kernel(dims, n_in, *refs):
    in_out, out_out = refs[-2:]
    pairs = list(zip(refs[0:-2:2], refs[1:-2:2]))
    length, _ = chunk_of(dims, dims.C)
    for h, (keep, got) in enumerate(pairs[:n_in]):
        rows = slice(0, length)
        in_out[pl.ds(h, length, stride=n_in), :] = keep[rows, :] + got[rows, :].astype(F32)
    first, length = 0, out_out.shape[0]
    for keep, got in pairs[n_in:]:
        count = min(keep.shape[0], length - first)
        out_out[first : first + count, :] = keep[:count, :] + got[:count, :].astype(F32)
        first += count


def call(dims, kernel, shapes, ins, scratch, cost, name, vmem=None):
    return pl.pallas_call(
        kernel,
        out_shape=shapes,
        in_specs=ins,
        out_specs=jax.tree.map(lambda _: pl.BlockSpec(memory_space=pltpu.VMEM), shapes),
        scratch_shapes=scratch,
        compiler_params=pltpu.CompilerParams(vmem_limit_bytes=vmem or dims.vmem),
        cost_estimate=pl.CostEstimate(flops=cost, bytes_accessed=4 << 20, transcendentals=0),
        name=name,
    )


def halving_steps(dims, order):
    steps = list(order)
    for axis, size in (("tm", dims.tm), ("rows", dims.rows)):
        apart = 4
        while apart < size:
            steps.append((axis, apart))
            apart *= 2
    steps = [(axis, apart, apart * (dims.rows if axis == "tm" else 1)) for axis, apart in steps]
    masks = [sum(s[2] for b, s in enumerate(steps) if m >> b & 1) for m in range(1 << len(steps))]
    return steps, masks


def group_swap(block, axis, apart):
    count = lax.axis_size(axis)
    return lax.ppermute(block, axis, [(i, i ^ apart) for i in range(count)])


def exchanged(blocks, n):
    got = lax.all_to_all(blocks.reshape(n, -1, blocks.shape[1]), ("tm", "rows"), 0, 0)
    return got.reshape(blocks.shape)


def edge_swap(dims, block, distance):
    pairs = []
    for k in range(dims.n):
        if 0 <= k + distance < dims.n:
            a, b = dims.slab_of(k), dims.n + dims.slab_of(k + distance)
            pairs += [(a, b), (b, a)]
    return lax.ppermute(block, ("segment", "tm", "rows"), pairs)


def added(dims, keep, send, step, name, also=None):
    got = group_swap(send, step[0], step[1])
    if also is not None:
        got, also = lax.optimization_barrier((got, also))
    half, rows, lanes = keep.shape
    vm = pl.BlockSpec(memory_space=pltpu.VMEM)
    shape = (half // 2, rows, lanes)
    keep, send = call(
        dims, add_kernel,
        (jax.ShapeDtypeStruct(shape, F32), jax.ShapeDtypeStruct(shape, BF)), [vm, vm], [], 0, name,
    )(keep, got)
    return keep, send, also


def on_device(shape, input_clip, cotangent, kernel_in, kernel_out):
    f_here, r_here, W, C = input_clip.shape
    D = kernel_in.shape[2]
    dims = Dims(shape, f_here, r_here, W, C, D)
    own, cell, n, fr = dims.own, dims.cell, dims.n, dims.fr
    kin, kout = kernel_in[0], kernel_out[0]
    kin_hbm, kout_hbm = (pltpu.with_memory_space_constraint(k, pltpu.HBM) for k in (kin, kout))
    vm = pl.BlockSpec(memory_space=pltpu.VMEM)
    hbm = pl.BlockSpec(memory_space=pltpu.HBM)
    sds = jax.ShapeDtypeStruct
    scr = pltpu.VMEM
    cols = own + 6
    conv_flops = 2 * 27 * C * D * cell
    e_cols, e_far = dims.edge(3)
    x_shape = sds(((own + 2) * cell, C), BF)
    a_shape = sds(((own + 2) * cell * (D // LANES), LANES), BF)

    send = call(
        dims, partial(pack_kernel, dims), sds((n * fr * cols, C), BF), [vm],
        [scr((fr, W + 16, C), F32), scr((n * fr * cols, C), F32)], 0, "pack",
    )(jnp.where(dims.my_role() == 0, input_clip, cotangent).reshape(fr, W, C))
    recv = exchanged(send, n)

    z, a1, x1, x1_lo, x1_hi, hd = call(
        dims, partial(first_kernel, dims),
        (
            x_shape, a_shape, sds((own * cell, C), BF), sds((e_cols * cell, C), BF),
            sds((e_cols * cell, C), BF), sds(((own + 4) * cell, D), F32),
        ),
        [vm, hbm, hbm],
        [
            scr(kin.shape, BF), scr(kout.shape, BF),
            scr((n * fr * cols, C), F32), scr((cols * cell, C), F32),
            scr((cols * cell, 9 * C), BF), scr(((own + 2) * cell, 9 * D), BF),
            scr((own * cell, C), F32), pltpu.SemaphoreType.DMA((2,)),
        ],
        conv_flops * 2 * (own + 2), "first",
    )(recv, kin_hbm, kout_hbm)

    x1_there = group_swap(x1, "segment", 1)
    lefts = [edge_swap(dims, x1_hi, far) for far in range(e_far, 0, -1)]
    rights = [edge_swap(dims, x1_lo, -far) for far in range(1, e_far + 1)]

    g0, x2, a2, e1 = call(
        dims, partial(second_kernel, dims, e_far),
        (x_shape, x_shape, a_shape, sds((own * cell, D), BF)),
        [vm] * (5 + 2 * e_far),
        [
            scr((cols * cell, 9 * C), BF), scr(((own + 4) * cell, 9 * D), BF),
            scr(((own + 2) * cell, C), F32),
            pltpu.SemaphoreType.DMA((2,)),
        ],
        conv_flops * 2 * (own + 2), "second",
    )(*lefts, x1_there, *rights, hd, z, a1, kin)

    g0_there = group_swap(g0, "segment", 1)
    a_beside = group_swap(a2, "rows", 1)
    x_beside = group_swap(x2, "rows", 1)

    e, g, sec = call(
        dims, partial(third_kernel, dims),
        (sds((own * cell, D), BF), sds((own * cell, C), BF), sds((n * fr * own, C), BF)),
        [vm] * 8,
        [
            scr(((own + 2) * cell, 9 * C), BF), scr(((own + 2) * cell, 9 * D), BF),
            scr((own * cell, C), F32),
            scr((n * fr * own, C), F32),
        ],
        conv_flops * own, "third",
    )(g0_there, hd, x1, z, x2, a2, e1, kout)
    e_beside = group_swap(e, "rows", 1)
    g_beside = group_swap(g, "rows", 1)

    in_steps, in_masks = halving_steps(dims, IN_ORDER)
    out_steps, out_masks = halving_steps(dims, OUT_ORDER)
    half = len(in_masks) // 2

    def grad(c, c_out, masks, v, v_beside, u, u_beside, name):
        shapes = []
        for rows, _ in streams_of(dims, c, c_out):
            shapes += [sds((half, rows, LANES), F32), sds((half, rows, LANES), BF)]
        sums = call(
            dims, partial(grad_kernel, dims, c, masks), tuple(shapes), [vm] * 4,
            [
                scr((2 * (own + 2) * cell, 9 * c), BF), scr((c_out, 2 * own * cell), BF),
                scr((27 * c + 64, c_out), F32),
            ],
            conv_flops * own, name,
        )(v, v_beside, u, u_beside)
        return [tuple(sums[at : at + 2]) for at in range(0, len(sums), 2)]

    out_parts = grad(D, C, out_masks, a2, a_beside, g, g_beside, "grad_out")
    e, e_beside, first_part = lax.optimization_barrier((e, e_beside, out_parts[0]))
    out_parts[0] = first_part
    in_parts = grad(C, D, in_masks, x2, x_beside, e, e_beside, "grad_in")
    back = None
    for at in range(len(in_steps) - 1):
        for parts, steps, name in (
            (out_parts, out_steps, "add_out"), (in_parts, in_steps, "add_in")
        ):
            for b, (keep, sent) in enumerate(parts):
                last = at == 1 and parts is in_parts and b == len(parts) - 1
                keep, sent, also = added(
                    dims, keep, sent, steps[at], name, back if last else None
                )
                back = also if last else back
                if at == 0 and parts is out_parts and b == 0:
                    sec, keep, sent = lax.optimization_barrier((sec, keep, sent))
                    back = exchanged(sec, n)
                parts[b] = (keep, sent)
    ends = []
    for parts, step in ((in_parts, in_steps[-1]), (out_parts, out_steps[-1])):
        for keep, sent in parts:
            ends += [keep[0], group_swap(sent[0], *step[:2])]
    shard = 27 * C * D // n // LANES
    in_sum, out_sum = call(
        dims, partial(final_kernel, dims, len(in_parts)), (sds((shard, LANES), F32),) * 2,
        [vm] * len(ends), [], 0, "final",
    )(*ends)

    sections = call(
        dims, partial(unpack_kernel, dims), sds((fr, W, C), BF), [vm],
        [scr((n * fr * own, C), F32), scr((fr, W, C), F32)], 0, "unpack",
    )(back).reshape(f_here, r_here, W, C)
    return sections[None], in_sum.reshape(1, -1), out_sum.reshape(1, -1)


def solution(mesh):
    in_specs = (
        P("tm", "rows", None, None),
        P("tm", "rows", None, None),
        P("segment", None, None),
        P("segment", None, None),
    )
    out_specs = (
        P("segment", "tm", "rows", None, None),
        P("segment", ("tm", "rows")),
        P("segment", ("tm", "rows")),
    )
    return jax.shard_map(
        partial(on_device, dict(mesh.shape)), mesh=mesh, in_specs=in_specs,
        out_specs=out_specs, check_vma=False,
    )
```
